512 devices in a mesh: segment: 16 (over y, core), tile: 32 (over z, x).
Axes of the slice: x: 4, y: 8, z: 8, core: 2. Of those that a mesh axis runs over, the one named last changes fastest.
Arguments:
- tile_mask_amplitude: bfloat16 [512, 256, 256], P('tile', 'segment'), may hold values from -4 to 4
- tile_target_images: bfloat16 [512, 256, 256], P('tile', 'segment'), may hold values from 0 to 1
- spectra: float32 [12, 2, 31, 31], replicated, may hold values from -6 to 6
- slot_dose_scale: float32 [512], P('tile'), may hold values from 0.5 to 2
- slot_row: int32 [512], P('tile'), may hold values from -1 to 31, as said below
- side_source: int32 [512, 2], P('tile'), may hold values from -1 to 11, as said below
Outputs:
- corrected_mask: bfloat16 [512, 256, 256], P('tile', 'segment')
- resist_image: float32 [512, 256, 256], P('tile', 'segment')
The draws below stay inside these ranges and needn't reach their ends.
Inputs may be any that keep to these rules, and one draw needn't show every extreme that they name: `slot_row`: in each tile owner's 16 slots the patterned tiles come first, with strictly rising tile rows below 32, and -1 marks the empty slots after them; every owner has at least 4 patterned tiles and at most 12, and some owner has exactly 12; every owner holds tile row 31. `side_source`: an entry names the slot of the neighbouring tile owner that holds the same tile row as this slot; it is -1 for empty slots, at the window's ends and where that tile is not patterned.
All inputs are finite; a program needn't handle non-finite values.
Results may differ from the reference program's by a relative error of at most 0.0075.
Values may be sent and summed in bfloat16 or wider, within the bound.
No kernel may reach another device: no remote copies, remote signals or barrier semaphores. Data moves between devices by JAX's collectives and lax.ppermute only.
A program may use at most 64 MiB of HBM per device.

```python
import math
import jax
import jax.numpy as jnp
from jax import lax

TILE_PIXELS = 256
KF = 31
NK = 12
RB = 8
ITERS = 2
OWNER_SLOTS = 16
TOTAL_SLOTS = 512


def tile_layout(key):
    rows_all = 2 * OWNER_SLOTS
    fullest_count = OWNER_SLOTS * 3 // 4
    tile_owners = TOTAL_SLOTS // OWNER_SLOTS
    count_key, pick_key, full_key = jax.random.split(jax.random.fold_in(key, 11), 3)
    counts = jax.random.randint(count_key, (tile_owners,), OWNER_SLOTS // 4, fullest_count + 1)
    fullest = jax.random.randint(full_key, (), 0, tile_owners)
    counts = jnp.where(jnp.arange(tile_owners) == fullest, fullest_count, counts).astype(jnp.int32)
    dev_keys = jax.random.split(pick_key, tile_owners)

    def one_owner(dev_key, owned):
        shuffled = jax.random.permutation(dev_key, rows_all - 1).astype(jnp.int32)
        shuffled = jnp.concatenate([shuffled, jnp.full((1,), rows_all - 1, jnp.int32)])
        row_index = jnp.arange(rows_all, dtype=jnp.int32)
        chosen = jnp.where(row_index < owned - 1, shuffled, rows_all + row_index)
        chosen = jnp.where(row_index == rows_all - 1, rows_all - 1, chosen)
        ranked = jnp.sort(chosen)[:OWNER_SLOTS]
        return jnp.where(jnp.arange(OWNER_SLOTS, dtype=jnp.int32) < owned, ranked, -1).astype(jnp.int32)
    rows_held = jax.vmap(one_owner)(dev_keys, counts)

    def match_rows(neighbour_rows):
        same_row = (rows_held[:, :, None] == neighbour_rows[:, None, :]) & (rows_held[:, :, None] >= 0)
        slot_number = jnp.arange(OWNER_SLOTS, dtype=jnp.int32) + 1
        return jnp.sum(jnp.where(same_row, slot_number[None, None, :], 0), axis=2).astype(jnp.int32) - 1
    no_owner = jnp.full((1, OWNER_SLOTS), -1, jnp.int32)
    before = jnp.concatenate([no_owner, rows_held[:-1]], 0)
    after_rows = jnp.concatenate([rows_held[1:], no_owner], 0)
    source = jnp.stack([match_rows(before), match_rows(after_rows)], 2)
    return (rows_held.reshape(-1), source.reshape(-1, 2).astype(jnp.int32))


def draw_slot_row(key, part):
    return tile_layout(key)[0]


def draw_side_source(key, part):
    return tile_layout(key)[1]


def block_scale(own_key, extent, cuts, low, largest):
    level, own = 1.0, jax.random.fold_in(own_key, 6)
    for dim, blocks in cuts:
        draws = jnp.exp(jax.random.uniform(jax.random.fold_in(own, dim), (blocks,), jnp.float32, low / len(cuts), largest / len(cuts)))
        level = level * jnp.repeat(draws, extent[dim] // blocks).reshape([-1 if axis == dim else 1 for axis in range(len(extent))])
    return level


def bell_draw(stream_key, shape, scale, reach, pieces=(), held_as=jnp.bfloat16):
    entries = scale * jax.random.normal(stream_key, shape, jnp.float32)
    if pieces:
        entries = entries * block_scale(stream_key, shape, pieces, -0.22, 0.18)
    return jnp.clip(entries, -reach, reach).astype(held_as)


def setup_inputs(seed: int = 0) -> dict:
    streams_of = jax.random.split(jax.random.key(seed), 7)
    return {
        "tile_mask_amplitude": bell_draw(streams_of[0], (TOTAL_SLOTS, TILE_PIXELS, TILE_PIXELS), 1.0, 4.0, ((0, 32), (1, 16))),
        "tile_target_images": jnp.clip(1.0 * jax.random.uniform(streams_of[1], (TOTAL_SLOTS, TILE_PIXELS, TILE_PIXELS), jnp.float32) ** block_scale(streams_of[1], (TOTAL_SLOTS, TILE_PIXELS, TILE_PIXELS), ((0, 32), (1, 16)), -0.2, 0.2), 0.0, 1.0).astype(jnp.bfloat16),
        "spectra": bell_draw(streams_of[2], (NK, 2, KF, KF), 1.0, 6.0, (), jnp.float32),
        "slot_dose_scale": jnp.clip(jnp.exp(math.log(2.0) - 1.3862944 * jax.random.uniform(streams_of[3], (TOTAL_SLOTS,), jnp.float32) ** block_scale(streams_of[3], (TOTAL_SLOTS,), ((0, 32),), -0.2, 0.2)), 0.5, 2.0),
        "slot_row": draw_slot_row(jax.random.fold_in(streams_of[6], 71), 0),
        "side_source": draw_side_source(jax.random.fold_in(streams_of[6], 71), 0),
    }


STEEPNESS = 1.5
THRESHOLD = 2.0
STEP_GAIN = 0.5

def wave_tables(length, freq_count):
    position = jnp.arange(length, dtype=jnp.int32)
    frequency = jnp.arange(freq_count, dtype=jnp.int32) - freq_count // 2
    phase_index = position[:, None] * frequency[None, :] % length
    angle_rad = phase_index.astype(jnp.float32) * jnp.float32(2.0 * math.pi / length)
    return (jnp.cos(angle_rad), jnp.sin(angle_rad))

def transform_tables(length, freq_count):
    cosine, sine_part = wave_tables(length, freq_count)
    norm_scale = jnp.float32(1.0 / math.sqrt(length))
    forward_cols = jnp.concatenate([cosine * norm_scale, -(sine_part * norm_scale)], 1).astype(jnp.bfloat16)
    forward_rows = jnp.concatenate([cosine * norm_scale, sine_part * norm_scale], 1).astype(jnp.bfloat16)
    inverse_rows = jnp.concatenate([cosine, sine_part], 1).astype(jnp.bfloat16)
    cosine_low = cosine.T.astype(jnp.bfloat16)
    sine_low = sine_part.T.astype(jnp.bfloat16)
    inverse_cols = jnp.concatenate([jnp.concatenate([cosine_low, sine_low], 1), jnp.concatenate([-sine_low, cosine_low], 1)], 0)
    return (forward_cols, forward_rows, inverse_rows, inverse_cols)

def blur_weights(radius):
    offsets = jnp.arange(2 * radius + 1, dtype=jnp.float32) - radius
    spread_width = radius / 2.0
    weights = jnp.exp(-offsets * offsets / (2.0 * spread_width * spread_width))
    return weights / jnp.sum(weights)

def tile_intensity(tile_item, spectra, tables):
    tile_data, weight_one = tile_item
    forward_cols, forward_rows, inverse_rows, inverse_cols = tables
    freq_count = spectra.shape[2]
    kernel_count = spectra.shape[0]
    tile_edge = tile_data.shape[1]
    y_part = jnp.dot(tile_data, forward_cols, preferred_element_type=jnp.float32).astype(jnp.bfloat16)
    inner = jnp.dot(forward_rows.T, y_part, preferred_element_type=jnp.float32)
    real_part = inner[:freq_count, :freq_count] + inner[freq_count:, freq_count:]
    imag_part = inner[:freq_count, freq_count:] - inner[freq_count:, :freq_count]
    spec_real = spectra[:, 0]
    spec_imag = spectra[:, 1]
    prod_real = (spec_real * real_part - spec_imag * imag_part).astype(jnp.bfloat16)
    prod_imag = (spec_real * imag_part + spec_imag * real_part).astype(jnp.bfloat16)
    right_block = jnp.concatenate([jnp.concatenate([prod_real, prod_imag], 2), jnp.concatenate([-prod_imag, prod_real], 2)], 1)
    field_a = jnp.einsum('ra,kab->krb', inverse_rows.astype(jnp.float32), right_block.astype(jnp.float32))
    field_a = (field_a * jnp.float32(1.0 / freq_count)).astype(jnp.bfloat16)
    field_full = jnp.einsum('krb,by->kry', field_a.astype(jnp.float32), inverse_cols.astype(jnp.float32))
    squares = lax.optimization_barrier(jnp.sum(field_full * field_full, axis=0))
    return (squares[:, :tile_edge] + squares[:, tile_edge:]) * jnp.float32(1.0 / kernel_count) * weight_one

def reference(tile_mask_amplitude, tile_target_images, spectra, slot_dose_scale, slot_row, side_source):
    slot_total, tile_edge, _ = tile_mask_amplitude.shape
    freq_count = spectra.shape[2]
    tables = transform_tables(tile_edge, freq_count)
    weights = blur_weights(RB)
    weight = slot_dose_scale * (slot_row >= 0).astype(jnp.float32)
    slot_index = jnp.arange(slot_total, dtype=jnp.int32)
    owner_index = slot_index // OWNER_SLOTS
    prev_row = jnp.concatenate([jnp.full((1,), -7, jnp.int32), slot_row[:-1]])
    up_ok = (slot_index % OWNER_SLOTS > 0) & (prev_row >= 0) & (slot_row >= 0) & (prev_row == slot_row - 1)
    down_ok = jnp.concatenate([up_ok[1:], jnp.zeros((1,), dtype=bool)])
    up_weight = up_ok.astype(jnp.float32)[:, None, None]
    down_weight = down_ok.astype(jnp.float32)[:, None, None]
    left_src = side_source[:, 0]
    right_src = side_source[:, 1]
    left_idx = jnp.clip((owner_index - 1) * OWNER_SLOTS + left_src, 0, slot_total - 1).astype(jnp.int32)
    right_idx = jnp.clip((owner_index + 1) * OWNER_SLOTS + right_src, 0, slot_total - 1).astype(jnp.int32)
    left_ok = (left_src >= 0).astype(jnp.float32)[:, None, None]
    right_ok = (right_src >= 0).astype(jnp.float32)[:, None, None]
    zero_rim = jnp.zeros((1, RB, tile_edge), jnp.float32)
    mask_now = tile_mask_amplitude
    resist = jnp.zeros((slot_total, tile_edge, tile_edge), jnp.float32)
    for sweep in range(ITERS):
        intensity = lax.map(lambda tile_item: tile_intensity(tile_item, spectra, tables), (mask_now, weight))
        right_edges = intensity[:, :, tile_edge - RB:]
        left_edges = intensity[:, :, :RB]
        left_band = right_edges[left_idx] * left_ok
        right_band = left_edges[right_idx] * right_ok
        padded = jnp.concatenate([left_band, intensity, right_band], 2)
        horiz_blur = weights[0] * padded[:, :, 0:tile_edge]
        for shift_by in range(1, 2 * RB + 1):
            horiz_blur = horiz_blur + weights[shift_by] * padded[:, :, shift_by:shift_by + tile_edge]
        upper_rim = jnp.concatenate([zero_rim, horiz_blur[:-1, tile_edge - RB:, :]], 0) * up_weight
        lower_rim = jnp.concatenate([horiz_blur[1:, :RB, :], zero_rim], 0) * down_weight
        vert_padded = jnp.concatenate([upper_rim, horiz_blur, lower_rim], 1)
        vert_blur = weights[0] * vert_padded[:, 0:tile_edge, :]
        for shift_by in range(1, 2 * RB + 1):
            vert_blur = vert_blur + weights[shift_by] * vert_padded[:, shift_by:shift_by + tile_edge, :]
        resist = jax.nn.sigmoid(STEEPNESS * (vert_blur - THRESHOLD))
        mask_now = (mask_now.astype(jnp.float32) + STEP_GAIN * (tile_target_images.astype(jnp.float32) - resist)).astype(jnp.bfloat16)
    return (mask_now, resist)
```

```python
import functools
import math

import jax
import jax.numpy as jnp
import ml_dtypes
import numpy as np
from jax import lax
from jax.experimental import pallas as pl
from jax.experimental.pallas import tpu as pltpu
from jax.sharding import PartitionSpec as P

EDGE = 256
KF = 31
NK = 12
RB = 8
ITERS = 2
SLOTS = 16
USED = 12
GROUPS = USED // 4
ROWS = 16
EXT = ROWS + 2 * RB
COARSE = 64
STEEPNESS = 1.5
THRESHOLD = 2.0
STEP_GAIN = 0.5
BF = jnp.bfloat16
F32 = jnp.float32


def bf16(x):
    return np.asarray(x, np.float32).astype(ml_dtypes.bfloat16)


def high_low(x):
    high = bf16(x)
    return high, bf16(np.asarray(x, np.float32) - high.astype(np.float32))


@functools.cache
def tables():
    freq = np.arange(32) - KF // 2
    live = (np.arange(32) < KF).astype(np.float64)

    def waves(position):
        angle = 2.0 * np.pi * ((np.asarray(position)[:, None] * freq[None, :]) % EDGE) / EDGE
        return np.cos(angle) * live, np.sin(angle) * live

    cos, sin = waves(np.arange(EDGE))
    t = {}
    t["cols"] = bf16(np.concatenate([np.tile(cos, (1, 4)), np.tile(-sin, (1, 4))], 1) / 16.0)
    t["rows"] = bf16(np.concatenate([cos, sin], 1).T / 16.0)
    ext_cos, ext_sin = waves((np.arange(EDGE + 2 * RB) - RB) % EDGE)
    t["ext"] = bf16(np.concatenate([ext_cos, ext_sin], 1))
    c_cos, c_sin = waves(np.arange(COARSE) * (EDGE // COARSE))
    inv = np.zeros((256, 512))
    for i in range(4):
        r, c = slice(32 * i, 32 * i + 32), 128 * i
        inv[r, c : c + 64] = c_cos.T
        inv[r, c + 64 : c + 128] = c_sin.T
        r = slice(128 + 32 * i, 128 + 32 * i + 32)
        inv[r, c : c + 64] = -c_sin.T
        inv[r, c + 64 : c + 128] = c_cos.T
    t["inv"] = bf16(inv)
    d = np.arange(EDGE)[None, :] - (EDGE // COARSE) * np.arange(COARSE)[:, None]
    interp = np.ones((COARSE, EDGE))
    for m in range(1, 32):
        interp += 2.0 * np.cos(2.0 * np.pi * m * d / EDGE)
    interp /= COARSE
    taps = np.exp(-(np.arange(-RB, RB + 1.0) ** 2) / (2.0 * (RB / 2.0) ** 2))
    taps /= taps.sum()
    blur = np.zeros((EDGE, EDGE))
    for a in range(EDGE):
        for b in range(max(0, a - RB), min(EDGE, a + RB + 1)):
            blur[a, b] = taps[a - b + RB]
    across = interp @ blur
    high, low = high_low(np.concatenate([across, across], 0))
    t["across"] = np.concatenate([high, low], 0)
    down = np.zeros((ROWS, EXT))
    for r in range(ROWS):
        down[r, r : r + 2 * RB + 1] = taps
    t["down"] = np.concatenate(high_low(down), 0)
    left = np.tile(np.concatenate([interp[:, :RB]] * 2, 0), (1, 16))
    right = np.tile(np.concatenate([interp[:, -RB:]] * 2, 0), (1, 16))
    t["band"] = bf16(np.concatenate([left, right], 1))
    w_left, w_right = np.zeros((RB, RB)), np.zeros((RB, RB))
    for c in range(RB):
        for q in range(RB):
            if c >= q:
                w_left[c, q] = taps[c - q]
            if c <= q:
                w_right[c, q] = taps[2 * RB + c - q]
    t["reach"] = np.concatenate([np.tile(w_left, (16, 16)), np.tile(w_right, (16, 16))], 1).astype(
        np.float32
    )
    return t


def dot(a, b):
    return jnp.dot(a, b, preferred_element_type=F32)


def lane_block(width, size):
    return lax.broadcasted_iota(jnp.int32, (1, width), 1) // size


def put_column_transform(mask, cols_ref, y_ref):
    both = dot(mask.reshape(USED * ROWS, EDGE), cols_ref[...])
    place = lane_block(256, 32) % 4
    for j in range(GROUPS):
        total = jnp.zeros((ROWS, 256), F32)
        for i in range(4):
            first = (4 * j + i) * ROWS
            total = jnp.where(place == i, both[first : first + ROWS], total)
        total = total.astype(BF)
        y_ref[:, 128 * j : 128 * (j + 1)] = total[:, :128]
        y_ref[:, 384 + 128 * j : 384 + 128 * (j + 1)] = total[:, 128:]


def start_kernel(mask_ref, spectra_ref, cols_ref, reach_ref, dose_ref, row_ref, side_ref,
                 y_ref, kernels_ref, slot_ref, small_ref, pick_ref):
    put_column_transform(mask_ref[:USED], cols_ref, y_ref)
    kernels_ref[...] = jnp.zeros_like(kernels_ref)
    for k in range(NK):
        for part in range(2):
            kernels_ref[k, part, :KF, :KF] = spectra_ref[k, part]
    for k in range(NK):
        for part in range(2):
            one = kernels_ref[k, part]
            one = one + pltpu.roll(one, 32, 1)
            kernels_ref[k, part] = one + pltpu.roll(one, 64, 1)
    wide, narrow = lane_block(128 * USED, 128), lane_block(128, RB)
    weight = jnp.zeros((1, 128 * USED), F32)
    up_wide, down_wide = weight, weight
    up_narrow = jnp.zeros((1, 128), F32)
    down_narrow = up_narrow
    left = jnp.full((1, 128), -1, jnp.int32)
    right = left
    for g in range(USED):
        row = row_ref[g]
        scale = jnp.where(row >= 0, dose_ref[g], 0.0) * (1.0 / (NK * KF * KF))
        weight = jnp.where(wide == g, scale, weight)
        if g > 0:
            before = row_ref[g - 1]
            joined = jnp.where((before >= 0) & (row >= 0) & (before == row - 1), 1.0, 0.0)
            up_wide = jnp.where(wide == g, joined, up_wide)
            down_wide = jnp.where(wide == g - 1, joined, down_wide)
            up_narrow = jnp.where(narrow == g, joined, up_narrow)
            down_narrow = jnp.where(narrow == g - 1, joined, down_narrow)
        left = jnp.where(narrow == g, side_ref[g, 0], left)
        right = jnp.where(narrow == g, side_ref[g, 1], right)
    slot_ref[...] = jnp.concatenate([weight, up_wide, down_wide, jnp.zeros((5, 128 * USED), F32)], 0)
    small_ref[...] = jnp.concatenate([up_narrow, down_narrow, jnp.zeros((6, 128), F32)], 0)
    source = lax.broadcasted_iota(jnp.int32, (128, 1), 0) // RB
    wanted = jnp.concatenate([left, right], 1)
    pick_ref[...] = jnp.where(source == wanted, reach_ref[...], 0.0).astype(BF)


def field_kernel(all_ref, rows_ref, kernels_ref, ext_ref, inv_ref, band_ref, slot_ref,
                 coarse_ref, to_left_ref, to_right_ref, held):
    first = pl.multiple_of(lax.axis_index("segment") * ROWS, ROWS)
    ext = ext_ref[pl.ds(first, EXT), :]
    inner = dot(rows_ref[...], all_ref[...])
    half = 32 * USED
    real = inner[:32, :half] + inner[32:, half:]
    imag = inner[:32, half:] - inner[32:, :half]
    place = lane_block(256, RB) % 16
    bands = jnp.zeros((EXT, 256), F32)
    for j in range(GROUPS):
        re, im = real[:, 128 * j : 128 * (j + 1)], imag[:, 128 * j : 128 * (j + 1)]
        for k in range(NK):
            k_re, k_im = kernels_ref[k, 0], kernels_ref[k, 1]
            p_re = k_re * re - k_im * im
            p_im = k_re * im + k_im * re
            block = jnp.concatenate(
                [jnp.concatenate([p_re, p_im], 1), jnp.concatenate([-p_im, p_re], 1)], 0
            ).astype(BF)
            held[j, k * EXT : (k + 1) * EXT, :] = dot(ext, block).astype(BF)
        field = dot(held[j], inv_ref[...])
        squares = jnp.sum((field * field).reshape(NK, EXT, 512), axis=0)
        squares = squares * slot_ref[0:1, 512 * j : 512 * (j + 1)]
        coarse_ref[:, 512 * j : 512 * (j + 1)] = squares
        low = squares.astype(BF)
        stack = jnp.concatenate([low[:, 128 * i : 128 * (i + 1)] for i in range(4)], 0)
        edges = dot(stack, band_ref[...])
        for i in range(4):
            bands = jnp.where(place == 4 * j + i, edges[EXT * i : EXT * (i + 1)], bands)
    to_left_ref[...] = bands[:, :128].astype(BF)
    to_right_ref[...] = bands[:, 128:].astype(BF)


def joined_rows(cells, up, down, step):
    segment = lax.axis_index("segment")
    top, middle, bottom = cells[:RB], cells[RB : RB + ROWS], cells[RB + ROWS :]
    top = jnp.where(segment == 0, pltpu.roll(top, step, 1) * up, top)
    width = cells.shape[1]
    bottom = jnp.where(
        segment == lax.axis_size("segment") - 1, pltpu.roll(bottom, width - step, 1) * down, bottom
    )
    return jnp.concatenate([top, middle, bottom], 0)


def blur_down(cells, down_ref):
    both = dot(down_ref[...], cells.astype(BF))
    return both[:ROWS] + both[ROWS:]


def blur_kernel(coarse_ref, slot_ref, down_ref, across_ref, inner_ref):
    cells = joined_rows(coarse_ref[...], slot_ref[1:2, :], slot_ref[2:3, :], 128)
    low = blur_down(cells, down_ref).astype(BF)
    stack = jnp.concatenate([low[:, 128 * g : 128 * (g + 1)] for g in range(USED)], 0)
    inner_ref[...] = dot(jnp.concatenate([stack, stack], 1), across_ref[...])


def update_kernel(last, inner_ref, from_left_ref, from_right_ref, pick_ref, small_ref, down_ref, cols_ref,
                  mask_ref, target_ref, new_ref, out_ref):
    up, down = small_ref[0:1, :], small_ref[1:2, :]
    lane = lax.broadcasted_iota(jnp.int32, (1, 128), 1)
    left = dot(from_left_ref[...], pick_ref[:, :128])
    right = dot(from_right_ref[...], pick_ref[:, 128:])
    left = blur_down(joined_rows(left, up, down, RB), down_ref)
    right = blur_down(joined_rows(right, up, down, RB), down_ref)
    for g in range(SLOTS):
        if g < USED:
            blurred = inner_ref[ROWS * g : ROWS * (g + 1), :]
            add_left = jnp.where(lane < RB, pltpu.roll(left, (128 - RB * g) % 128, 1), 0.0)
            add_right = jnp.where(lane >= 128 - RB, pltpu.roll(right, 128 - RB - RB * g, 1), 0.0)
            blurred = blurred + jnp.concatenate([add_left, add_right], 1)
        else:
            blurred = jnp.zeros((ROWS, EDGE), F32)
        resist = jax.nn.sigmoid(STEEPNESS * (blurred - THRESHOLD))
        if last:
            out_ref[g] = resist
        step = STEP_GAIN * (target_ref[g].astype(F32) - resist)
        new_ref[g] = (mask_ref[g].astype(F32) + step).astype(BF)
    if not last:
        put_column_transform(new_ref[:USED], cols_ref, out_ref)


VMEM = pl.BlockSpec(memory_space=pltpu.VMEM)
SMEM = pl.BlockSpec(memory_space=pltpu.SMEM)


def call(kernel, ins, outs, flops, scratch=(), name=None):
    size = sum(math.prod(o.shape) * o.dtype.itemsize for o in outs)
    return pl.pallas_call(
        kernel,
        out_shape=tuple(outs),
        in_specs=list(ins),
        out_specs=tuple(VMEM for _ in outs),
        scratch_shapes=list(scratch),
        compiler_params=pltpu.CompilerParams(vmem_limit_bytes=32 * 2**20),
        cost_estimate=pl.CostEstimate(flops=flops, bytes_accessed=2 * size, transcendentals=0),
        name=name,
    )


def passed_along(block, distance):
    devices = range(lax.axis_size("tile"))
    route = [(i - distance, i) for i in devices if i - distance in devices]
    return lax.ppermute(block, "tile", route)


def body(mask, target, spectra, dose, slot_row, side_source):
    t = {name: jnp.asarray(value) for name, value in tables().items()}
    shape = jax.ShapeDtypeStruct
    y_shape = shape((ROWS, 64 * USED), BF)
    y, kernels, slot, small, pick = call(
        start_kernel,
        [VMEM, VMEM, VMEM, VMEM, SMEM, SMEM, SMEM],
        [y_shape, shape((NK, 2, 32, 128), F32), shape((8, 128 * USED), F32), shape((8, 128), F32), shape((128, 256), BF)],
        10**8,
        name="start",
    )(mask, spectra, t["cols"], t["reach"], dose, slot_row, side_source)
    for sweep in range(ITERS):
        last = sweep == ITERS - 1
        rows_all = lax.all_gather(y, "segment", axis=0, tiled=True)
        coarse, to_left, to_right = call(
            field_kernel,
            [VMEM] * 7,
            [shape((EXT, 128 * USED), F32), shape((EXT, 128), BF), shape((EXT, 128), BF)],
            10**9,
            [pltpu.VMEM((GROUPS, NK * EXT, 256), BF)],
            name="fields",
        )(rows_all, t["rows"], kernels, t["ext"], t["inv"], t["band"], slot)
        from_left = passed_along(to_right, 1)
        from_right = passed_along(to_left, -1)
        (inner,) = call(
            blur_kernel, [VMEM] * 4, [shape((USED * ROWS, EDGE), F32)], 10**9, name="blur"
        )(coarse, slot, t["down"], t["across"])
        out = shape((SLOTS, ROWS, EDGE), F32) if last else y_shape
        mask, result = call(
            functools.partial(update_kernel, last),
            [VMEM] * 9,
            [shape((SLOTS, ROWS, EDGE), BF), out],
            10**8,
            name="update",
        )(inner, from_left, from_right, pick, small, t["down"], t["cols"], mask, target)
        y = result
    return mask, result


def solution(mesh):
    in_specs = (
        P("tile", "segment", None),
        P("tile", "segment", None),
        P(),
        P("tile"),
        P("tile"),
        P("tile", None),
    )
    out_specs = (P("tile", "segment", None), P("tile", "segment", None))
    return jax.shard_map(body, mesh=mesh, in_specs=in_specs, out_specs=out_specs, check_vma=False)
```

```python
import functools
import math

import jax
import jax.numpy as jnp
import ml_dtypes
import numpy as np
from jax import lax
from jax.experimental import pallas as pl
from jax.experimental.pallas import tpu as pltpu
from jax.sharding import PartitionSpec as P

EDGE = 256
KF = 31
NK = 12
RB = 8
SLOTS = 16
USED = 12
GROUPS = USED // 4
ROWS = 16
EXT = ROWS + 2 * RB
COARSE = 64
STEEPNESS = 1.5
THRESHOLD = 2.0
STEP_GAIN = 0.5
BF = jnp.bfloat16
F32 = jnp.float32


def bf16(x):
    return np.asarray(x, np.float32).astype(ml_dtypes.bfloat16)


def high_low(x):
    high = bf16(x)
    return high, bf16(np.asarray(x, np.float32) - high.astype(np.float32))


@functools.cache
def tables():
    freq = np.arange(32) - KF // 2
    live = (np.arange(32) < KF).astype(np.float64)

    def waves(position):
        angle = 2.0 * np.pi * ((np.asarray(position)[:, None] * freq[None, :]) % EDGE) / EDGE
        return np.cos(angle) * live, np.sin(angle) * live

    cos, sin = waves(np.arange(EDGE))
    t = {}
    t["cols"] = bf16(np.concatenate([np.tile(cos, (1, 4)), np.tile(-sin, (1, 4))], 1) / 16.0)
    t["rows"] = bf16(np.concatenate([cos, sin], 1).T / 16.0)
    ext_cos, ext_sin = waves((np.arange(EDGE + 2 * RB) - RB) % EDGE)
    t["ext"] = bf16(np.concatenate([ext_cos, ext_sin], 1))
    c_cos, c_sin = waves(np.arange(COARSE) * (EDGE // COARSE))
    t["grid"] = bf16(np.concatenate([c_cos, c_sin], 1))
    inv = np.zeros((256, 512))
    for i in range(4):
        r, c = slice(32 * i, 32 * i + 32), 128 * i
        inv[r, c : c + 64] = c_cos.T
        inv[r, c + 64 : c + 128] = c_sin.T
        r = slice(128 + 32 * i, 128 + 32 * i + 32)
        inv[r, c : c + 64] = -c_sin.T
        inv[r, c + 64 : c + 128] = c_cos.T
    t["inv"] = bf16(inv)
    d = np.arange(EDGE)[None, :] - (EDGE // COARSE) * np.arange(COARSE)[:, None]
    interp = np.ones((COARSE, EDGE))
    for m in range(1, 32):
        interp += 2.0 * np.cos(2.0 * np.pi * m * d / EDGE)
    interp /= COARSE
    taps = np.exp(-(np.arange(-RB, RB + 1.0) ** 2) / (2.0 * (RB / 2.0) ** 2))
    taps /= taps.sum()
    blur = np.zeros((EDGE, EDGE))
    above = np.zeros((EDGE, EDGE))
    below = np.zeros((EDGE, EDGE))
    for b in range(EDGE):
        for step in range(-RB, RB + 1):
            a = b + step
            (above if a < 0 else below if a >= EDGE else blur)[a % EDGE, b] += taps[step + RB]
    across = np.zeros((128, EDGE))
    across[:COARSE] = interp @ blur
    across[COARSE : COARSE + RB] = above[EDGE - RB :]
    across[COARSE + RB : COARSE + 2 * RB] = below[:RB]
    t["across"] = np.concatenate(high_low(across), 0)
    main_high, main_low = high_low((interp @ blur).T)
    t["tall"] = np.concatenate(
        [main_high, bf16((interp @ above).T), bf16((interp @ below).T), main_low], 1
    )
    down = np.zeros((ROWS, EXT))
    for r in range(ROWS):
        down[r, r : r + 2 * RB + 1] = taps
    t["down"] = np.concatenate(high_low(down), 0)
    band = np.zeros((128, 256))
    band[:COARSE, :128] = np.tile(interp[:, :RB], (1, 16))
    band[:COARSE, 128:] = np.tile(interp[:, -RB:], (1, 16))
    t["band"] = bf16(band)
    return t


def dot(a, b):
    return jnp.dot(a, b, preferred_element_type=F32)


def lane_block(width, size):
    return lax.broadcasted_iota(jnp.int32, (1, width), 1) // size


def four_slots(blocks, place):
    total = blocks[0]
    for i in range(1, 4):
        total = jnp.where(place == i, blocks[i], total)
    return total


def start_kernel(mask_ref, target_ref, spectra_ref, cols_ref, dose_ref, row_ref, side_ref,
                 y_ref, kernels_ref, slot_ref, pick_ref):
    of_mask = dot(mask_ref[:USED].reshape(USED * ROWS, EDGE), cols_ref[...])
    of_target = dot(target_ref[:USED].reshape(USED * ROWS, EDGE), cols_ref[...])
    place = lane_block(256, 32) % 4
    for n, both in enumerate((of_mask, of_mask + STEP_GAIN * of_target)):
        for j in range(GROUPS):
            firsts = [(4 * j + i) * ROWS for i in range(4)]
            total = four_slots([both[f : f + ROWS] for f in firsts], place).astype(BF)
            lane = 768 * n + 128 * j
            y_ref[:, lane : lane + 128] = total[:, :128]
            y_ref[:, lane + 384 : lane + 512] = total[:, 128:]
    kernels_ref[...] = jnp.zeros_like(kernels_ref)
    for k in range(NK):
        for part in range(2):
            kernels_ref[k, part, :KF, :KF] = spectra_ref[pl.ds(2 * KF * k + part, KF, stride=2), :]
    for k in range(NK):
        for part in range(2):
            one = kernels_ref[k, part]
            one = one + pltpu.roll(one, 32, 1)
            kernels_ref[k, part] = one + pltpu.roll(one, 64, 1)
    wide, narrow = lane_block(128 * USED, 128), lane_block(256, 2 * RB)
    weight = jnp.zeros((1, 128 * USED), F32)
    up, down = weight, weight
    wanted = jnp.full((1, 256), -1, jnp.int32)
    is_left = lane_block(256, RB) % 2 == 0
    for g in range(USED):
        row = row_ref[g]
        scale = jnp.where(row >= 0, dose_ref[g], 0.0) * (1.0 / (NK * KF * KF))
        weight = jnp.where(wide == g, scale, weight)
        if g > 0:
            before = row_ref[g - 1]
            joined = jnp.where((before >= 0) & (row >= 0) & (before == row - 1), 1.0, 0.0)
            up = jnp.where(wide == g, joined, up)
            down = jnp.where(wide == g - 1, joined, down)
        wanted = jnp.where(narrow == g, jnp.where(is_left, side_ref[0, g], side_ref[1, g]), wanted)
    slot_ref[...] = jnp.concatenate([weight, up, down, jnp.zeros((5, 128 * USED), F32)], 0)
    here = lax.broadcasted_iota(jnp.int32, (256, 1), 0)
    lane = lax.broadcasted_iota(jnp.int32, (1, 256), 1)
    match = ((here % 128) // RB == wanted) & (here % RB == lane % RB) & ((here < 128) == is_left)
    pick_ref[...] = jnp.where(match, 1.0, 0.0).astype(BF)


def intensities(inner, kernels_ref, points, inv_ref, band_ref, slot_ref, held, coarse_ref, to_left_ref, to_right_ref):
    count = points.shape[0]
    place = lane_block(256, RB) % 16
    bands = jnp.zeros((count, 256), F32)
    for j in range(GROUPS):
        total = inner(j)
        re = total[:32, :128] + total[32:, 128:]
        im = total[:32, 128:] - total[32:, :128]
        for k in range(NK):
            k_re, k_im = kernels_ref[k, 0], kernels_ref[k, 1]
            p_re = k_re * re - k_im * im
            p_im = k_re * im + k_im * re
            block = jnp.concatenate(
                [jnp.concatenate([p_re, p_im], 1), jnp.concatenate([-p_im, p_re], 1)], 0
            ).astype(BF)
            held[j, k * count : (k + 1) * count, :] = dot(points, block).astype(BF)
        field = dot(held[j], inv_ref[...])
        squares = jnp.sum((field * field).reshape(NK, count, 512), axis=0)
        squares = squares * slot_ref[0:1, 512 * j : 512 * (j + 1)]
        parts = [squares[:, 128 * i : 128 * (i + 1)] for i in range(4)]
        parts = [(part + pltpu.roll(part, COARSE, 1)).astype(BF) for part in parts]
        for i in range(4):
            first = 128 * (4 * j + i)
            coarse_ref[:, first : first + 128] = parts[i]
        edges = dot(jnp.concatenate(parts, 0), band_ref[...])
        for i in range(4):
            bands = jnp.where(place == 4 * j + i, edges[count * i : count * (i + 1)], bands)
    to_left_ref[...] = bands[:, :128].astype(BF)
    to_right_ref[...] = bands[:, 128:].astype(BF)


def field_kernel(all_ref, rows_ref, kernels_ref, grid_ref, inv_ref, band_ref, slot_ref,
                 coarse_ref, to_left_ref, to_right_ref, base_ref, held):
    inner = dot(rows_ref[...], all_ref[...])
    base_ref[...] = inner[:, 768:]
    half = 32 * USED

    def group(j):
        return jnp.concatenate(
            [inner[:, 128 * j : 128 * (j + 1)], inner[:, half + 128 * j : half + 128 * (j + 1)]], 1
        )

    intensities(group, kernels_ref, grid_ref[...], inv_ref, band_ref, slot_ref, held,
                coarse_ref, to_left_ref, to_right_ref)


def side_lanes(from_left_ref, from_right_ref, pick_ref):
    received = jnp.concatenate([from_left_ref[...], from_right_ref[...]], 1)
    picked = dot(received, pick_ref[...])
    lane = lax.broadcasted_iota(jnp.int32, (1, 128), 1)
    inside = (lane >= COARSE) & (lane < COARSE + 2 * RB)
    parts = []
    for g in range(USED):
        part = picked[:, 128 * (g // 8) : 128 * (g // 8) + 128]
        part = pltpu.roll(part, (COARSE - 2 * RB * (g % 8)) % 128, 1)
        parts.append(jnp.where(inside, part, 0.0))
    return jnp.concatenate(parts, 1)


def own_lanes(coarse):
    return jnp.where(lax.broadcasted_iota(jnp.int32, (1, 128 * USED), 1) % 128 < COARSE, coarse, 0.0)


def middle_kernel(coarse_ref, from_left_ref, from_right_ref, pick_ref, slot_ref, tall_ref, across_ref,
                  rows_ref, cols_ref, base_ref, kernels_ref, ext_ref, inv_ref, band_ref,
                  mine_ref, next_ref, to_left_ref, to_right_ref, blurred, turned, held):
    cells = own_lanes(coarse_ref[...].astype(F32)) + side_lanes(from_left_ref, from_right_ref, pick_ref)
    above = pltpu.roll(cells, 128, 1) * slot_ref[1:2, :]
    below = pltpu.roll(cells, 128 * (USED - 1), 1) * slot_ref[2:3, :]
    main = cells.astype(BF)
    blurred[...] = dot(tall_ref[...], jnp.concatenate([main, above.astype(BF), below.astype(BF), main], 0)).astype(BF)
    first = pl.multiple_of(lax.axis_index("segment") * ROWS, ROWS)
    mine_ref[...] = blurred[pl.ds(first, ROWS), :]
    for g in range(USED):
        one = blurred[:, 128 * g : 128 * (g + 1)]
        fine = dot(jnp.concatenate([one, one], 1), across_ref[...])
        resist = resist_of(fine).astype(BF)
        turned[64 * g : 64 * (g + 1), :] = dot(rows_ref[...], resist).astype(BF)
    both = dot(turned[...], cols_ref[...])
    place = lane_block(256, 32) % 4
    half = 32 * USED

    def group(j):
        total = four_slots([both[64 * (4 * j + i) : 64 * (4 * j + i + 1)] for i in range(4)], place)
        base = jnp.concatenate(
            [base_ref[:, 128 * j : 128 * (j + 1)], base_ref[:, half + 128 * j : half + 128 * (j + 1)]], 1
        )
        return base - STEP_GAIN * total

    ext = ext_ref[pl.ds(first, EXT), :]
    intensities(group, kernels_ref, ext, inv_ref, band_ref, slot_ref, held, next_ref, to_left_ref, to_right_ref)


def resist_of(blurred):
    return 0.5 * jnp.tanh((0.5 * STEEPNESS) * (blurred - THRESHOLD)) + 0.5


def stacked(low):
    stack = jnp.concatenate([low[:, 128 * g : 128 * (g + 1)] for g in range(USED)], 0)
    return jnp.concatenate([stack, stack], 1)


def blur_rows(cells, slot_ref, down_ref):
    segment = lax.axis_index("segment")
    top, center, bottom = cells[:RB], cells[RB : RB + ROWS], cells[RB + ROWS :]
    top = jnp.where(segment == 0, pltpu.roll(top, 128, 1) * slot_ref[1:2, :], top)
    bottom = jnp.where(
        segment == lax.axis_size("segment") - 1,
        pltpu.roll(bottom, 128 * (USED - 1), 1) * slot_ref[2:3, :],
        bottom,
    )
    both = dot(down_ref[...], jnp.concatenate([top, center, bottom], 0).astype(BF))
    return (both[:ROWS] + both[ROWS:]).astype(BF)


def local_kernel(mine_ref, coarse_ref, slot_ref, down_ref, across_ref, mask_ref, target_ref, inner_ref, once_ref):
    resist = resist_of(dot(stacked(mine_ref[...]), across_ref[...]))
    for g in range(SLOTS):
        part = resist[ROWS * g : ROWS * (g + 1)] if g < USED else resist_of(jnp.zeros((ROWS, EDGE), F32))
        once_ref[g] = (mask_ref[g].astype(F32) + STEP_GAIN * (target_ref[g].astype(F32) - part)).astype(BF)
    cells = own_lanes(coarse_ref[...].astype(F32))
    inner_ref[...] = dot(stacked(blur_rows(cells, slot_ref, down_ref)), across_ref[...])


def final_kernel(inner_ref, from_left_ref, from_right_ref, pick_ref, slot_ref, down_ref, across_ref,
                 once_ref, target_ref, mask_ref, resist_ref):
    sides = blur_rows(side_lanes(from_left_ref, from_right_ref, pick_ref), slot_ref, down_ref)
    blurred = inner_ref[...] + dot(stacked(sides), across_ref[...])
    for g in range(SLOTS):
        part = resist_of(blurred[ROWS * g : ROWS * (g + 1)] if g < USED else jnp.zeros((ROWS, EDGE), F32))
        resist_ref[g] = part
        mask_ref[g] = (once_ref[g].astype(F32) + STEP_GAIN * (target_ref[g].astype(F32) - part)).astype(BF)


VMEM = pl.BlockSpec(memory_space=pltpu.VMEM)
SMEM = pl.BlockSpec(memory_space=pltpu.SMEM)


def call(kernel, ins, outs, flops, scratch=(), name=None):
    size = sum(math.prod(o.shape) * o.dtype.itemsize for o in outs)
    return pl.pallas_call(
        kernel,
        out_shape=tuple(outs),
        in_specs=list(ins),
        out_specs=tuple(VMEM for _ in outs),
        scratch_shapes=list(scratch),
        compiler_params=pltpu.CompilerParams(vmem_limit_bytes=32 * 2**20),
        cost_estimate=pl.CostEstimate(flops=flops, bytes_accessed=2 * size, transcendentals=0),
        name=name,
    )


def passed_along(block, distance):
    devices = range(lax.axis_size("tile"))
    route = [(i - distance, i) for i in devices if i - distance in devices]
    return lax.ppermute(block, "tile", route)


def body(mask, target, spectra, dose, slot_row, side_source):
    t = {name: jnp.asarray(value) for name, value in tables().items()}
    shape = jax.ShapeDtypeStruct
    plane = spectra.transpose(0, 2, 1, 3).reshape(NK * KF * 2, KF)
    y, kernels, slot, pick = call(
        start_kernel,
        [VMEM] * 4 + [SMEM] * 3,
        [
            shape((ROWS, 128 * USED), BF),
            shape((NK, 2, 32, 128), F32),
            shape((8, 128 * USED), F32),
            shape((256, 256), BF),
        ],
        10**8,
        name="start",
    )(mask, target, plane, t["cols"], dose, slot_row, side_source.T)
    rows_all = lax.all_gather(y, "segment", axis=0, tiled=True)
    coarse, to_left, to_right, base = call(
        field_kernel,
        [VMEM] * 7,
        [
            shape((COARSE, 128 * USED), BF),
            shape((COARSE, 128), BF),
            shape((COARSE, 128), BF),
            shape((64, 64 * USED), F32),
        ],
        10**9,
        [pltpu.VMEM((GROUPS, NK * COARSE, 256), BF)],
        name="fields",
    )(rows_all, t["rows"], kernels, t["grid"], t["inv"], t["band"], slot)
    from_left = passed_along(to_right, 1)
    from_right = passed_along(to_left, -1)
    mine, coarse, to_left, to_right = call(
        middle_kernel,
        [VMEM] * 14,
        [
            shape((ROWS, 128 * USED), BF),
            shape((EXT, 128 * USED), BF),
            shape((EXT, 128), BF),
            shape((EXT, 128), BF),
        ],
        10**9,
        [
            pltpu.VMEM((EDGE, 128 * USED), BF),
            pltpu.VMEM((64 * USED, EDGE), BF),
            pltpu.VMEM((GROUPS, NK * EXT, 256), BF),
        ],
        name="middle",
    )(coarse, from_left, from_right, pick, slot, t["tall"], t["across"], t["rows"], t["cols"], base,
      kernels, t["ext"], t["inv"], t["band"])
    from_left = passed_along(to_right, 1)
    from_right = passed_along(to_left, -1)
    inner, once = call(
        local_kernel,
        [VMEM] * 7,
        [shape((USED * ROWS, EDGE), F32), shape((SLOTS, ROWS, EDGE), BF)],
        10**9,
        name="local",
    )(mine, coarse, slot, t["down"], t["across"], mask, target)
    return call(
        final_kernel,
        [VMEM] * 9,
        [shape((SLOTS, ROWS, EDGE), BF), shape((SLOTS, ROWS, EDGE), F32)],
        10**8,
        name="final",
    )(inner, from_left, from_right, pick, slot, t["down"], t["across"], once, target)


def solution(mesh):
    in_specs = (
        P("tile", "segment", None),
        P("tile", "segment", None),
        P(),
        P("tile"),
        P("tile"),
        P("tile", None),
    )
    out_specs = (P("tile", "segment", None), P("tile", "segment", None))
    return jax.shard_map(body, mesh=mesh, in_specs=in_specs, out_specs=out_specs, check_vma=False)
```

```python
import functools
import math

import jax
import jax.numpy as jnp
import ml_dtypes
import numpy as np
from jax import lax
from jax.experimental import pallas as pl
from jax.experimental.pallas import tpu as pltpu
from jax.sharding import PartitionSpec as P

EDGE = 256
KF = 31
NK = 12
RB = 8
SLOTS = 16
USED = 12
GROUPS = USED // 4
ROWS = 16
EXT = ROWS + 2 * RB
COARSE = 64
STEEPNESS = 1.5
THRESHOLD = 2.0
STEP_GAIN = 0.5
BF = jnp.bfloat16
F32 = jnp.float32


def bf16(x):
    return np.asarray(x, np.float32).astype(ml_dtypes.bfloat16)


def high_low(x):
    high = bf16(x)
    return high, bf16(np.asarray(x, np.float32) - high.astype(np.float32))


@functools.cache
def tables():
    freq = np.arange(32) - KF // 2
    live = (np.arange(32) < KF).astype(np.float64)

    def waves(position):
        angle = 2.0 * np.pi * ((np.asarray(position)[:, None] * freq[None, :]) % EDGE) / EDGE
        return np.cos(angle) * live, np.sin(angle) * live

    cos, sin = waves(np.arange(EDGE))
    t = {}
    t["cols"] = bf16(np.concatenate([np.tile(cos, (1, 4)), np.tile(-sin, (1, 4))], 1) / 16.0)
    t["rows"] = bf16(np.concatenate([cos, sin], 1).T / 16.0)
    ext_cos, ext_sin = waves((np.arange(EDGE + 2 * RB) - RB) % EDGE)
    t["ext"] = bf16(np.concatenate([ext_cos, ext_sin], 1))
    c_cos, c_sin = waves(np.arange(COARSE) * (EDGE // COARSE))
    t["grid"] = bf16(np.concatenate([c_cos, c_sin], 1))
    inv = np.zeros((256, 512))
    for i in range(4):
        r, c = slice(32 * i, 32 * i + 32), 128 * i
        inv[r, c : c + 64] = c_cos.T
        inv[r, c + 64 : c + 128] = c_sin.T
        r = slice(128 + 32 * i, 128 + 32 * i + 32)
        inv[r, c : c + 64] = -c_sin.T
        inv[r, c + 64 : c + 128] = c_cos.T
    t["inv"] = bf16(inv)
    d = np.arange(EDGE)[None, :] - (EDGE // COARSE) * np.arange(COARSE)[:, None]
    interp = np.ones((COARSE, EDGE))
    for m in range(1, 32):
        interp += 2.0 * np.cos(2.0 * np.pi * m * d / EDGE)
    interp /= COARSE
    taps = np.exp(-(np.arange(-RB, RB + 1.0) ** 2) / (2.0 * (RB / 2.0) ** 2))
    taps /= taps.sum()
    blur = np.zeros((EDGE, EDGE))
    above = np.zeros((EDGE, EDGE))
    below = np.zeros((EDGE, EDGE))
    for b in range(EDGE):
        for step in range(-RB, RB + 1):
            a = b + step
            (above if a < 0 else below if a >= EDGE else blur)[a % EDGE, b] += taps[step + RB]
    wide = np.concatenate([interp @ blur] * 2, 0)
    t["across"] = np.concatenate(high_low(wide), 0)
    side = np.concatenate([np.arange(RB), np.arange(EDGE - RB, EDGE)])
    own = np.zeros((128 * USED, 256))
    for g in range(USED):
        own[128 * g : 128 * (g + 1), 16 * g : 16 * (g + 1)] = wide[:, side]
    t["own"] = bf16(own)
    full = np.concatenate([np.tile(cos, (1, 4)), np.tile(-sin, (1, 4))], 1) / 16.0
    inside = full.copy()
    inside[side] = 0.0
    t["inside"] = bf16(inside)
    rim = np.zeros((256, 768))
    for g in range(USED):
        rim[16 * g : 16 * (g + 1), 32 * g : 32 * g + 32] = cos[side] / 16.0
        rim[16 * g : 16 * (g + 1), 384 + 32 * g : 384 + 32 * g + 32] = -sin[side] / 16.0
    t["rim"] = bf16(rim)
    e_cos, e_sin = waves(side)
    inv_side = np.zeros((256, 128))
    for i in range(4):
        r, c = slice(32 * i, 32 * i + 32), 32 * i
        inv_side[r, c : c + 16] = e_cos.T
        inv_side[r, c + 16 : c + 32] = e_sin.T
        r = slice(128 + 32 * i, 128 + 32 * i + 32)
        inv_side[r, c : c + 16] = -e_sin.T
        inv_side[r, c + 16 : c + 32] = e_cos.T
    t["inv_side"] = bf16(inv_side)
    reach = np.zeros((512, 256))
    for n in range(512):
        q = n % 16
        if n % 256 >= 128 + 128 or (n % 256 >= 128 and (n // 16) % 2):
            continue
        for p in range(16):
            if n < 256 and q >= 8 and p < 8:
                reach[n, p::16] = above[EDGE - RB + q - 8, p]
            if n >= 256 and q < 8 and p >= 8:
                reach[n, p::16] = below[q, EDGE - RB + p - 8]
    t["reach"] = bf16(reach)
    main_high, main_low = high_low((interp @ blur).T)
    t["tall"] = np.concatenate(
        [main_high, bf16((interp @ above).T), bf16((interp @ below).T), main_low], 1
    )
    down = np.zeros((ROWS, EXT))
    for r in range(ROWS):
        down[r, r : r + 2 * RB + 1] = taps
    t["down"] = np.concatenate(high_low(down), 0)
    return t


def dot(a, b):
    return jnp.dot(a, b, preferred_element_type=F32)


def lane_block(width, size):
    return lax.broadcasted_iota(jnp.int32, (1, width), 1) // size


def four_slots(blocks, place):
    total = blocks[0]
    for i in range(1, 4):
        total = jnp.where(place == i, blocks[i], total)
    return total


def start_kernel(mask_hbm, target_hbm, cols_hbm, y_ref, mask_ref, target_ref, cols_ref, sems):
    copies = [
        pltpu.make_async_copy(mask_hbm.at[pl.ds(0, USED)], mask_ref, sems.at[0]),
        pltpu.make_async_copy(cols_hbm, cols_ref, sems.at[1]),
        pltpu.make_async_copy(target_hbm.at[pl.ds(0, USED)], target_ref, sems.at[2]),
    ]
    for copy in copies:
        copy.start()
    for copy in copies:
        copy.wait()
    of_mask = dot(mask_ref[...].reshape(USED * ROWS, EDGE), cols_ref[...])
    of_target = dot(target_ref[...].reshape(USED * ROWS, EDGE), cols_ref[...])
    place = lane_block(256, 32) % 4
    for n, both in enumerate((of_mask, of_mask + STEP_GAIN * of_target)):
        for j in range(GROUPS):
            firsts = [(4 * j + i) * ROWS for i in range(4)]
            total = four_slots([both[f : f + ROWS] for f in firsts], place).astype(BF)
            lane = 768 * n + 128 * j
            y_ref[:, lane : lane + 128] = total[:, :128]
            y_ref[:, lane + 384 : lane + 512] = total[:, 128:]


def lay_kernels(plane_ref, kernels_ref):
    kernels_ref[...] = jnp.zeros_like(kernels_ref)
    for k in range(NK):
        for part in range(2):
            kernels_ref[k, part, :KF, :KF] = plane_ref[pl.ds(2 * KF * k + part, KF, stride=2), :]
    for k in range(NK):
        for part in range(2):
            one = kernels_ref[k, part]
            one = one + pltpu.roll(one, 32, 1)
            kernels_ref[k, part] = one + pltpu.roll(one, 64, 1)


def lay_slots(dose_ref, row_ref, slot_ref, narrow_ref):
    wide, narrow, quarter = lane_block(128 * USED, 128), lane_block(256, 2 * RB), lane_block(128 * GROUPS, 32)
    weight, up, down = (jnp.zeros((1, 128 * USED), F32) for _ in range(3))
    up_narrow, down_narrow = (jnp.zeros((1, 256), F32) for _ in range(2))
    weight_quarter = jnp.zeros((1, 128 * GROUPS), F32)
    for g in range(USED):
        row = row_ref[g]
        scale = jnp.where(row >= 0, dose_ref[g], 0.0) * (1.0 / (NK * KF * KF))
        weight = jnp.where(wide == g, scale, weight)
        weight_quarter = jnp.where(quarter == g, scale, weight_quarter)
        if g > 0:
            before = row_ref[g - 1]
            joined = jnp.where((before >= 0) & (row >= 0) & (before == row - 1), 1.0, 0.0)
            up = jnp.where(wide == g, joined, up)
            down = jnp.where(wide == g - 1, joined, down)
            up_narrow = jnp.where(narrow == g, joined, up_narrow)
            down_narrow = jnp.where(narrow == g - 1, joined, down_narrow)
    slot_ref[...] = jnp.concatenate([weight, up, down, jnp.zeros((5, 128 * USED), F32)], 0)
    narrow_ref[...] = jnp.concatenate(
        [
            jnp.concatenate([up_narrow, jnp.zeros((1, 128), F32)], 1),
            jnp.concatenate([down_narrow, jnp.zeros((1, 128), F32)], 1),
            weight_quarter,
            jnp.zeros((5, 128 * GROUPS), F32),
        ],
        0,
    )


def lay_pick(side_ref, reach_ref, pick_ref):
    narrow = lane_block(256, 2 * RB)
    row = lax.broadcasted_iota(jnp.int32, (256, 1), 0)
    source = jnp.where(row < 128, row // 32 + 4 * ((row // 16) % 2), 8 + (row - 128) // 32)
    for n in range(2):
        wanted = jnp.full((1, 256), -1, jnp.int32)
        for g in range(USED):
            wanted = jnp.where(narrow == g, side_ref[n, g], wanted)
        rows = slice(256 * n, 256 * (n + 1))
        pick_ref[rows, :] = jnp.where(source == wanted, reach_ref[rows, :].astype(F32), 0.0).astype(BF)


def side_columns(inner, kernels_ref, points, inv_side_ref, narrow_ref, held, bands_ref):
    count = points.shape[0]
    half = 32 * USED
    sides = []
    for j in range(GROUPS):
        lanes, more = slice(128 * j, 128 * (j + 1)), slice(half + 128 * j, half + 128 * (j + 1))
        re = inner[:32, lanes] + inner[32:, more]
        im = inner[:32, more] - inner[32:, lanes]
        for k in range(NK):
            k_re, k_im = kernels_ref[k, 0], kernels_ref[k, 1]
            p_re = k_re * re - k_im * im
            p_im = k_re * im + k_im * re
            block = jnp.concatenate(
                [jnp.concatenate([p_re, p_im], 1), jnp.concatenate([-p_im, p_re], 1)], 0
            ).astype(BF)
            held[j, k * count : (k + 1) * count, :] = dot(points, block).astype(BF)
        field = dot(held[j], inv_side_ref[...])
        squares = jnp.sum((field * field).reshape(NK, count, 128), axis=0)
        sides.append((squares + pltpu.roll(squares, 112, 1)) * narrow_ref[2:3, lanes])
    even = lane_block(128, 16) % 2 == 0
    bands_ref[:, :128] = jnp.where(even, sides[0], pltpu.roll(sides[1], 16, 1)).astype(BF)
    bands_ref[:, 128:] = jnp.where(even, sides[2], 0.0).astype(BF)


def coarse_group(held, j, count, inv_ref, slot_ref):
    field = dot(held[j], inv_ref[...])
    squares = jnp.sum((field * field).reshape(NK, count, 512), axis=0)
    return squares * slot_ref[0:1, 512 * j : 512 * (j + 1)]


def first_kernel(all_ref, rows_ref, plane_ref, grid_ref, inv_side_ref, dose_ref, row_ref,
                 held_ref, bands_ref, base_ref, kernels_ref, slot_ref, narrow_ref):
    lay_kernels(plane_ref, kernels_ref)
    lay_slots(dose_ref, row_ref, slot_ref, narrow_ref)
    inner = dot(rows_ref[...], all_ref[...])
    base_ref[...] = inner[:, 768:]
    side_columns(inner[:, :768], kernels_ref, grid_ref[...], inv_side_ref, narrow_ref, held_ref, bands_ref)


def inside_kernel(held_ref, inv_ref, slot_ref, tall_ref, across_ref, rows_ref, inside_ref, base_ref, own_ref,
                  reach_ref, side_ref, part_ref, edge_ref, mine_ref, pick_ref, cells_ref, blurred, turned):
    lay_pick(side_ref, reach_ref, pick_ref)
    for j in range(GROUPS):
        cells_ref[:, 512 * j : 512 * (j + 1)] = coarse_group(held_ref, j, COARSE, inv_ref, slot_ref)
    cells = cells_ref[...]
    above = pltpu.roll(cells, 128, 1) * slot_ref[1:2, :]
    below = pltpu.roll(cells, 128 * (USED - 1), 1) * slot_ref[2:3, :]
    main = cells.astype(BF)
    edge_ref[...] = dot(main, own_ref[...])
    blurred[...] = dot(tall_ref[...], jnp.concatenate([main, above.astype(BF), below.astype(BF), main], 0)).astype(BF)
    first = pl.multiple_of(lax.axis_index("segment") * ROWS, ROWS)
    mine_ref[...] = blurred[pl.ds(first, ROWS), :]
    for g in range(USED):
        one = blurred[:, 128 * g : 128 * (g + 1)]
        fine = dot(jnp.concatenate([one, one], 1), across_ref[...])
        turned[64 * g : 64 * (g + 1), :] = dot(rows_ref[...], resist_of(fine).astype(BF)).astype(BF)
    both = dot(turned[...], inside_ref[...])
    place = lane_block(256, 32) % 4
    half = 32 * USED
    for j in range(GROUPS):
        total = four_slots([both[64 * (4 * j + i) : 64 * (4 * j + i + 1)] for i in range(4)], place)
        for n, first_lane in enumerate((128 * j, half + 128 * j)):
            lanes = slice(first_lane, first_lane + 128)
            part_ref[:, lanes] = base_ref[:, lanes] - STEP_GAIN * total[:, 128 * n : 128 * (n + 1)]


def lent(from_left_ref, from_right_ref, pick_ref):
    return dot(jnp.concatenate([from_left_ref[...], from_right_ref[...]], 1), pick_ref[...])


def second_kernel(from_left_ref, from_right_ref, pick_ref, edge_ref, narrow_ref, tall_ref, rows_ref, rim_ref, part_ref,
                  kernels_ref, ext_ref, inv_side_ref, held_ref, bands_ref, mine_side_ref, blurred):
    cells = edge_ref[...] + lent(from_left_ref, from_right_ref, pick_ref)
    above = pltpu.roll(cells, 2 * RB, 1) * narrow_ref[0:1, :256]
    below = pltpu.roll(cells, 256 - 2 * RB, 1) * narrow_ref[1:2, :256]
    main = cells.astype(BF)
    fine = dot(tall_ref[...], jnp.concatenate([main, above.astype(BF), below.astype(BF), main], 0))
    blurred[...] = fine
    first = pl.multiple_of(lax.axis_index("segment") * ROWS, ROWS)
    mine_side_ref[...] = blurred[pl.ds(first, ROWS), :]
    turned = dot(rows_ref[...], resist_of(fine).astype(BF)).astype(BF)
    inner = part_ref[...] - STEP_GAIN * dot(turned, rim_ref[...])
    side_columns(inner, kernels_ref, ext_ref[pl.ds(first, EXT), :], inv_side_ref, narrow_ref, held_ref, bands_ref)


def resist_of(blurred):
    return 0.5 * jnp.tanh((0.5 * STEEPNESS) * (blurred - THRESHOLD)) + 0.5


def stacked(low):
    stack = jnp.concatenate([low[:, 128 * g : 128 * (g + 1)] for g in range(USED)], 0)
    return jnp.concatenate([stack, stack], 1)


def blur_rows(cells, up, down, step, down_ref):
    segment = lax.axis_index("segment")
    width = cells.shape[1]
    top, center, bottom = cells[:RB], cells[RB : RB + ROWS], cells[RB + ROWS :]
    top = jnp.where(segment == 0, pltpu.roll(top, step, 1) * up, top)
    bottom = jnp.where(
        segment == lax.axis_size("segment") - 1, pltpu.roll(bottom, width - step, 1) * down, bottom
    )
    both = dot(down_ref[...], jnp.concatenate([top, center, bottom], 0).astype(BF))
    return both[:ROWS] + both[ROWS:]


def at_sides(narrow, g):
    part = narrow[:, 128 * (g // 8) : 128 * (g // 8) + 128]
    first = 2 * RB * (g % 8)
    return pltpu.roll(part, (128 - first) % 128, 1), pltpu.roll(part, (112 - first) % 128, 1)


def local_kernel(mine_ref, mine_side_ref, held_ref, inv_ref, slot_ref, down_ref, across_ref, mask_ref, target_ref,
                 inner_ref, once_ref, cells_ref):
    fine = dot(stacked(mine_ref[...]), across_ref[...])
    lane = lax.broadcasted_iota(jnp.int32, (1, 128), 1)
    mine_side = mine_side_ref[...]
    for g in range(SLOTS):
        if g < USED:
            left, right = at_sides(mine_side, g)
            part = fine[ROWS * g : ROWS * (g + 1)]
            left = jnp.where(lane < RB, left, part[:, :128])
            right = jnp.where(lane >= 128 - RB, right, part[:, 128:])
            part = jnp.concatenate([left, right], 1)
        else:
            part = jnp.zeros((ROWS, EDGE), F32)
        step = STEP_GAIN * (target_ref[g].astype(F32) - resist_of(part))
        once_ref[g] = (mask_ref[g].astype(F32) + step).astype(BF)
    for j in range(GROUPS):
        cells_ref[:, 512 * j : 512 * (j + 1)] = coarse_group(held_ref, j, EXT, inv_ref, slot_ref)
    low = blur_rows(cells_ref[...], slot_ref[1:2, :], slot_ref[2:3, :], 128, down_ref)
    inner_ref[...] = dot(stacked(low.astype(BF)), across_ref[...])


def final_kernel(inner_ref, from_left_ref, from_right_ref, pick_ref, narrow_ref, down_ref, once_ref, target_ref,
                 mask_hbm, resist_hbm, mask_ref, resist_ref, sems):
    def sent(n):
        four = pl.ds(4 * n, 4)
        return [
            pltpu.make_async_copy(resist_ref.at[four], resist_hbm.at[four], sems.at[n]),
            pltpu.make_async_copy(mask_ref.at[four], mask_hbm.at[four], sems.at[4 + n]),
        ]

    lane = lax.broadcasted_iota(jnp.int32, (1, 128), 1)
    for n in (3, 0, 1, 2):
        if n == 0:
            narrow = blur_rows(lent(from_left_ref, from_right_ref, pick_ref), narrow_ref[0:1, :256],
                               narrow_ref[1:2, :256], 2 * RB, down_ref)
        for g in range(4 * n, 4 * n + 4):
            if g < USED:
                left, right = at_sides(narrow, g)
                left = jnp.where(lane < RB, left, 0.0)
                right = jnp.where(lane >= 128 - RB, right, 0.0)
                part = inner_ref[ROWS * g : ROWS * (g + 1), :] + jnp.concatenate([left, right], 1)
            else:
                part = jnp.zeros((ROWS, EDGE), F32)
            part = resist_of(part)
            resist_ref[g] = part
            mask_ref[g] = (once_ref[g].astype(F32) + STEP_GAIN * (target_ref[g].astype(F32) - part)).astype(BF)
        for copy in sent(n):
            copy.start()
    for n in range(4):
        for copy in sent(n):
            copy.wait()


VMEM = pl.BlockSpec(memory_space=pltpu.VMEM)
SMEM = pl.BlockSpec(memory_space=pltpu.SMEM)
HBM = pl.BlockSpec(memory_space=pltpu.HBM)


def call(kernel, ins, outs, flops, scratch=(), name=None, place=VMEM, grant=32 * 2**20):
    size = sum(math.prod(o.shape) * o.dtype.itemsize for o in outs)
    return pl.pallas_call(
        kernel,
        out_shape=tuple(outs),
        in_specs=list(ins),
        out_specs=tuple(place for _ in outs),
        scratch_shapes=list(scratch),
        compiler_params=pltpu.CompilerParams(vmem_limit_bytes=grant),
        cost_estimate=pl.CostEstimate(flops=flops, bytes_accessed=2 * size, transcendentals=0),
        name=name,
    )


def passed_along(block, distance):
    devices = range(lax.axis_size("tile"))
    route = [(i - distance, i) for i in devices if i - distance in devices]
    return lax.ppermute(block, "tile", route)


def body(mask, target, spectra, dose, slot_row, side_source):
    t = {name: jnp.asarray(value) for name, value in tables().items()}
    shape = jax.ShapeDtypeStruct
    tile_rows = pltpu.VMEM((USED, ROWS, EDGE), BF)
    plane = spectra.transpose(0, 2, 1, 3).reshape(NK * KF * 2, KF)
    (y,) = call(
        start_kernel,
        [HBM] * 3,
        [shape((ROWS, 128 * USED), BF)],
        10**8,
        [tile_rows, tile_rows, pltpu.VMEM((EDGE, 256), BF), pltpu.SemaphoreType.DMA((3,))],
        name="start",
        grant=62 * 2**20,
    )(mask, target, t["cols"])
    rows_all = lax.all_gather(y, "segment", axis=0, tiled=True)
    held, bands, base, kernels, slot, narrow = call(
        first_kernel,
        [VMEM] * 5 + [SMEM] * 2,
        [
            shape((GROUPS, NK * COARSE, 256), BF),
            shape((COARSE, 256), BF),
            shape((64, 64 * USED), F32),
            shape((NK, 2, 32, 128), F32),
            shape((8, 128 * USED), F32),
            shape((8, 128 * GROUPS), F32),
        ],
        10**9,
        name="first",
    )(rows_all, t["rows"], plane, t["grid"], t["inv_side"], dose, slot_row)
    from_left = passed_along(bands, 1)
    from_right = passed_along(bands, -1)
    part, edge, mine, pick = call(
        inside_kernel,
        [VMEM] * 10 + [SMEM],
        [
            shape((64, 64 * USED), F32),
            shape((COARSE, 256), F32),
            shape((ROWS, 128 * USED), BF),
            shape((512, 256), BF),
        ],
        10**9,
        [
            pltpu.VMEM((COARSE, 128 * USED), F32),
            pltpu.VMEM((EDGE, 128 * USED), BF),
            pltpu.VMEM((64 * USED, EDGE), BF),
        ],
        name="inside",
    )(held, t["inv"], slot, t["tall"], t["across"], t["rows"], t["inside"], base, t["own"], t["reach"], side_source.T)
    held, bands, mine_side = call(
        second_kernel,
        [VMEM] * 12,
        [shape((GROUPS, NK * EXT, 256), BF), shape((EXT, 256), BF), shape((ROWS, 256), F32)],
        10**9,
        [pltpu.VMEM((EDGE, 256), F32)],
        name="second",
    )(from_left, from_right, pick, edge, narrow, t["tall"], t["rows"], t["rim"], part, kernels, t["ext"], t["inv_side"])
    from_left = passed_along(bands, 1)
    from_right = passed_along(bands, -1)
    inner, once = call(
        local_kernel,
        [VMEM] * 9,
        [shape((USED * ROWS, EDGE), F32), shape((SLOTS, ROWS, EDGE), BF)],
        10**9,
        [pltpu.VMEM((EXT, 128 * USED), F32)],
        name="local",
    )(mine, mine_side, held, t["inv"], slot, t["down"], t["across"], mask, target)
    return call(
        final_kernel,
        [VMEM] * 8,
        [shape((SLOTS, ROWS, EDGE), BF), shape((SLOTS, ROWS, EDGE), F32)],
        10**8,
        [
            pltpu.VMEM((SLOTS, ROWS, EDGE), BF),
            pltpu.VMEM((SLOTS, ROWS, EDGE), F32),
            pltpu.SemaphoreType.DMA((8,)),
        ],
        name="final",
        place=HBM,
    )(inner, from_left, from_right, pick, narrow, t["down"], once, target)


def solution(mesh):
    in_specs = (
        P("tile", "segment", None),
        P("tile", "segment", None),
        P(),
        P("tile"),
        P("tile"),
        P("tile", None),
    )
    out_specs = (P("tile", "segment", None), P("tile", "segment", None))
    return jax.shard_map(body, mesh=mesh, in_specs=in_specs, out_specs=out_specs, check_vma=False)
```

```python
import functools
import math

import jax
import jax.numpy as jnp
import ml_dtypes
import numpy as np
from jax import lax
from jax.experimental import pallas as pl
from jax.experimental.pallas import tpu as pltpu
from jax.sharding import PartitionSpec as P

EDGE = 256
KF = 31
NK = 12
RB = 8
SLOTS = 16
USED = 12
GROUPS = USED // 4
ROWS = 16
EXT = ROWS + 2 * RB
COARSE = 64
STEEPNESS = 1.5
THRESHOLD = 2.0
STEP_GAIN = 0.5
BF = jnp.bfloat16
F32 = jnp.float32


def bf16(x):
    return np.asarray(x, np.float32).astype(ml_dtypes.bfloat16)


def high_low(x):
    high = bf16(x)
    return high, bf16(np.asarray(x, np.float32) - high.astype(np.float32))


@functools.cache
def tables():
    freq = np.arange(32) - KF // 2
    live = (np.arange(32) < KF).astype(np.float64)

    def waves(position):
        angle = 2.0 * np.pi * ((np.asarray(position)[:, None] * freq[None, :]) % EDGE) / EDGE
        return np.cos(angle) * live, np.sin(angle) * live

    cos, sin = waves(np.arange(EDGE))
    t = {}
    t["cols"] = bf16(np.concatenate([np.tile(cos, (1, 4)), np.tile(-sin, (1, 4))], 1) / 16.0)
    t["rows"] = bf16(np.concatenate([cos, sin], 1).T / 16.0)
    ext_cos, ext_sin = waves((np.arange(EDGE + 2 * RB) - RB) % EDGE)
    t["ext"] = bf16(np.concatenate([ext_cos, ext_sin], 1))
    c_cos, c_sin = waves(np.arange(COARSE) * (EDGE // COARSE))
    t["grid"] = bf16(np.concatenate([c_cos, c_sin], 1))
    inv = np.zeros((256, 512))
    for i in range(4):
        r, c = slice(32 * i, 32 * i + 32), 128 * i
        inv[r, c : c + 64] = c_cos.T
        inv[r, c + 64 : c + 128] = c_sin.T
        r = slice(128 + 32 * i, 128 + 32 * i + 32)
        inv[r, c : c + 64] = -c_sin.T
        inv[r, c + 64 : c + 128] = c_cos.T
    t["inv"] = bf16(inv)
    d = np.arange(EDGE)[None, :] - (EDGE // COARSE) * np.arange(COARSE)[:, None]
    interp = np.ones((COARSE, EDGE))
    for m in range(1, 32):
        interp += 2.0 * np.cos(2.0 * np.pi * m * d / EDGE)
    interp /= COARSE
    taps = np.exp(-(np.arange(-RB, RB + 1.0) ** 2) / (2.0 * (RB / 2.0) ** 2))
    taps /= taps.sum()
    blur = np.zeros((EDGE, EDGE))
    above = np.zeros((EDGE, EDGE))
    below = np.zeros((EDGE, EDGE))
    for b in range(EDGE):
        for step in range(-RB, RB + 1):
            a = b + step
            (above if a < 0 else below if a >= EDGE else blur)[a % EDGE, b] += taps[step + RB]
    wide = np.concatenate([interp @ blur] * 2, 0)
    t["across"] = np.concatenate(high_low(wide), 0)
    side = np.concatenate([np.arange(RB), np.arange(EDGE - RB, EDGE)])
    own = np.zeros((128 * USED, 256))
    for g in range(USED):
        own[128 * g : 128 * (g + 1), 16 * g : 16 * (g + 1)] = wide[:, side]
    t["own"] = bf16(own)
    full = np.concatenate([np.tile(cos, (1, 4)), np.tile(-sin, (1, 4))], 1) / 16.0
    inside = full.copy()
    inside[side] = 0.0
    t["inside"] = bf16(inside)
    rim = np.zeros((256, 768))
    for g in range(USED):
        rim[16 * g : 16 * (g + 1), 32 * g : 32 * g + 32] = cos[side] / 16.0
        rim[16 * g : 16 * (g + 1), 384 + 32 * g : 384 + 32 * g + 32] = -sin[side] / 16.0
    t["rim"] = bf16(rim)
    e_cos, e_sin = waves(side)
    inv_side = np.zeros((256, 128))
    for i in range(4):
        r, c = slice(32 * i, 32 * i + 32), 32 * i
        inv_side[r, c : c + 16] = e_cos.T
        inv_side[r, c + 16 : c + 32] = e_sin.T
        r = slice(128 + 32 * i, 128 + 32 * i + 32)
        inv_side[r, c : c + 16] = -e_sin.T
        inv_side[r, c + 16 : c + 32] = e_cos.T
    t["inv_side"] = bf16(inv_side)
    reach = np.zeros((512, 256))
    for n in range(512):
        q = n % 16
        if n % 256 >= 128 + 128 or (n % 256 >= 128 and (n // 16) % 2):
            continue
        for p in range(16):
            if n < 256 and q >= 8 and p < 8:
                reach[n, p::16] = above[EDGE - RB + q - 8, p]
            if n >= 256 and q < 8 and p >= 8:
                reach[n, p::16] = below[q, EDGE - RB + p - 8]
    t["reach"] = bf16(reach)
    main_high, main_low = high_low((interp @ blur).T)
    t["tall"] = np.concatenate(
        [main_high, bf16((interp @ above).T), bf16((interp @ below).T), main_low], 1
    )
    down = np.zeros((ROWS, EXT))
    for r in range(ROWS):
        down[r, r : r + 2 * RB + 1] = taps
    t["down"] = np.concatenate(high_low(down), 0)
    return t


def dot(a, b):
    return jnp.dot(a, b, preferred_element_type=F32)


def lane_block(width, size):
    return lax.broadcasted_iota(jnp.int32, (1, width), 1) // size


def four_slots(blocks, place):
    total = blocks[0]
    for i in range(1, 4):
        total = jnp.where(place == i, blocks[i], total)
    return total


def start_kernel(mask_hbm, target_hbm, cols_hbm, y_ref, mask_ref, target_ref, cols_ref, sems):
    copies = [
        pltpu.make_async_copy(mask_hbm.at[pl.ds(0, USED)], mask_ref, sems.at[0]),
        pltpu.make_async_copy(cols_hbm, cols_ref, sems.at[1]),
        pltpu.make_async_copy(target_hbm.at[pl.ds(0, USED)], target_ref, sems.at[2]),
    ]
    for copy in copies:
        copy.start()
    for copy in copies:
        copy.wait()
    of_mask = dot(mask_ref[...].reshape(USED * ROWS, EDGE), cols_ref[...])
    of_target = dot(target_ref[...].reshape(USED * ROWS, EDGE), cols_ref[...])
    place = lane_block(256, 32) % 4
    for n, both in enumerate((of_mask, of_mask + STEP_GAIN * of_target)):
        for j in range(GROUPS):
            firsts = [(4 * j + i) * ROWS for i in range(4)]
            total = four_slots([both[f : f + ROWS] for f in firsts], place).astype(BF)
            lane = 768 * n + 128 * j
            y_ref[:, lane : lane + 128] = total[:, :128]
            y_ref[:, lane + 384 : lane + 512] = total[:, 128:]


def lay_kernels(plane_ref, kernels_ref):
    kernels_ref[...] = jnp.zeros_like(kernels_ref)
    for k in range(NK):
        for part in range(2):
            kernels_ref[k, part, :KF, :KF] = plane_ref[pl.ds(2 * KF * k + part, KF, stride=2), :]
    for k in range(NK):
        for part in range(2):
            one = kernels_ref[k, part]
            one = one + pltpu.roll(one, 32, 1)
            kernels_ref[k, part] = one + pltpu.roll(one, 64, 1)


def lay_slots(dose_ref, row_ref, slot_ref, narrow_ref):
    wide, narrow, quarter = lane_block(128 * USED, 128), lane_block(256, 2 * RB), lane_block(128 * GROUPS, 32)
    weight, up, down = (jnp.zeros((1, 128 * USED), F32) for _ in range(3))
    up_narrow, down_narrow = (jnp.zeros((1, 256), F32) for _ in range(2))
    weight_quarter = jnp.zeros((1, 128 * GROUPS), F32)
    for g in range(USED):
        row = row_ref[g]
        scale = jnp.where(row >= 0, dose_ref[g], 0.0) * (1.0 / (NK * KF * KF))
        weight = jnp.where(wide == g, scale, weight)
        weight_quarter = jnp.where(quarter == g, scale, weight_quarter)
        if g > 0:
            before = row_ref[g - 1]
            joined = jnp.where((before >= 0) & (row >= 0) & (before == row - 1), 1.0, 0.0)
            up = jnp.where(wide == g, joined, up)
            down = jnp.where(wide == g - 1, joined, down)
            up_narrow = jnp.where(narrow == g, joined, up_narrow)
            down_narrow = jnp.where(narrow == g - 1, joined, down_narrow)
    slot_ref[...] = jnp.concatenate([weight, up, down, jnp.zeros((5, 128 * USED), F32)], 0)
    narrow_ref[...] = jnp.concatenate(
        [
            jnp.concatenate([up_narrow, jnp.zeros((1, 128), F32)], 1),
            jnp.concatenate([down_narrow, jnp.zeros((1, 128), F32)], 1),
            weight_quarter,
            jnp.zeros((5, 128 * GROUPS), F32),
        ],
        0,
    )


def lay_pick(side_ref, reach_ref, pick_ref):
    narrow = lane_block(256, 2 * RB)
    row = lax.broadcasted_iota(jnp.int32, (256, 1), 0)
    source = jnp.where(row < 128, row // 32 + 4 * ((row // 16) % 2), 8 + (row - 128) // 32)
    for n in range(2):
        wanted = jnp.full((1, 256), -1, jnp.int32)
        for g in range(USED):
            wanted = jnp.where(narrow == g, side_ref[n, g], wanted)
        rows = slice(256 * n, 256 * (n + 1))
        pick_ref[rows, :] = jnp.where(source == wanted, reach_ref[rows, :].astype(F32), 0.0).astype(BF)


def side_columns(inner, kernels_ref, points, inv_side_ref, narrow_ref, held, bands_ref):
    count = points.shape[0]
    half = 32 * USED
    sides = []
    for j in range(GROUPS):
        lanes, more = slice(128 * j, 128 * (j + 1)), slice(half + 128 * j, half + 128 * (j + 1))
        re = inner[:32, lanes] + inner[32:, more]
        im = inner[:32, more] - inner[32:, lanes]
        for k in range(NK):
            k_re, k_im = kernels_ref[k, 0], kernels_ref[k, 1]
            p_re = k_re * re - k_im * im
            p_im = k_re * im + k_im * re
            block = jnp.concatenate(
                [jnp.concatenate([p_re, p_im], 1), jnp.concatenate([-p_im, p_re], 1)], 0
            ).astype(BF)
            held[j, k * count : (k + 1) * count, :] = dot(points, block).astype(BF)
        field = dot(held[j], inv_side_ref[...])
        squares = jnp.sum((field * field).reshape(NK, count, 128), axis=0)
        sides.append((squares + pltpu.roll(squares, 112, 1)) * narrow_ref[2:3, lanes])
    even = lane_block(128, 16) % 2 == 0
    bands_ref[:, :128] = jnp.where(even, sides[0], pltpu.roll(sides[1], 16, 1)).astype(BF)
    bands_ref[:, 128:] = jnp.where(even, sides[2], 0.0).astype(BF)


def coarse_group(held, j, count, inv_ref, slot_ref):
    field = dot(held[j], inv_ref[...])
    squares = jnp.sum((field * field).reshape(NK, count, 512), axis=0)
    return squares * slot_ref[0:1, 512 * j : 512 * (j + 1)]


def first_kernel(all_ref, rows_ref, plane_ref, grid_ref, inv_side_ref, dose_ref, row_ref,
                 held_ref, bands_ref, base_ref, kernels_ref, slot_ref, narrow_ref):
    lay_kernels(plane_ref, kernels_ref)
    lay_slots(dose_ref, row_ref, slot_ref, narrow_ref)
    inner = dot(rows_ref[...], all_ref[...])
    base_ref[...] = inner[:, 768:]
    side_columns(inner[:, :768], kernels_ref, grid_ref[...], inv_side_ref, narrow_ref, held_ref, bands_ref)


def inside_kernel(held_ref, inv_ref, slot_ref, tall_ref, across_ref, rows_ref, inside_ref, base_ref, own_ref,
                  reach_ref, side_ref, part_ref, edge_ref, mine_ref, pick_ref, cells_ref, blurred, turned):
    lay_pick(side_ref, reach_ref, pick_ref)
    for j in range(GROUPS):
        cells_ref[:, 512 * j : 512 * (j + 1)] = coarse_group(held_ref, j, COARSE, inv_ref, slot_ref)
    cells = cells_ref[...]
    above = pltpu.roll(cells, 128, 1) * slot_ref[1:2, :]
    below = pltpu.roll(cells, 128 * (USED - 1), 1) * slot_ref[2:3, :]
    main = cells.astype(BF)
    edge_ref[...] = dot(main, own_ref[...])
    blurred[...] = dot(tall_ref[...], jnp.concatenate([main, above.astype(BF), below.astype(BF), main], 0)).astype(BF)
    first = pl.multiple_of(lax.axis_index("segment") * ROWS, ROWS)
    mine_ref[...] = blurred[pl.ds(first, ROWS), :]
    for g in range(USED):
        one = blurred[:, 128 * g : 128 * (g + 1)]
        fine = dot(jnp.concatenate([one, one], 1), across_ref[...])
        turned[64 * g : 64 * (g + 1), :] = dot(rows_ref[...], resist_of(fine).astype(BF)).astype(BF)
    both = dot(turned[...], inside_ref[...])
    place = lane_block(256, 32) % 4
    half = 32 * USED
    for j in range(GROUPS):
        total = four_slots([both[64 * (4 * j + i) : 64 * (4 * j + i + 1)] for i in range(4)], place)
        for n, first_lane in enumerate((128 * j, half + 128 * j)):
            lanes = slice(first_lane, first_lane + 128)
            part_ref[:, lanes] = base_ref[:, lanes] - STEP_GAIN * total[:, 128 * n : 128 * (n + 1)]


def lent(near_ref, far_ref, pick_ref):
    odd = lax.axis_index("tile") % 2 == 1
    far, near = far_ref[...].astype(F32), near_ref[...].astype(F32)
    left, right = jnp.where(odd, near, far), jnp.where(odd, far, near)
    return dot(jnp.concatenate([left, right], 1).astype(BF), pick_ref[...])


def second_kernel(near_ref, far_ref, pick_ref, edge_ref, narrow_ref, tall_ref, rows_ref, rim_ref, part_ref,
                  kernels_ref, ext_ref, inv_side_ref, held_ref, bands_ref, mine_side_ref, blurred):
    cells = edge_ref[...] + lent(near_ref, far_ref, pick_ref)
    above = pltpu.roll(cells, 2 * RB, 1) * narrow_ref[0:1, :256]
    below = pltpu.roll(cells, 256 - 2 * RB, 1) * narrow_ref[1:2, :256]
    main = cells.astype(BF)
    fine = dot(tall_ref[...], jnp.concatenate([main, above.astype(BF), below.astype(BF), main], 0))
    blurred[...] = fine
    first = pl.multiple_of(lax.axis_index("segment") * ROWS, ROWS)
    mine_side_ref[...] = blurred[pl.ds(first, ROWS), :]
    turned = dot(rows_ref[...], resist_of(fine).astype(BF)).astype(BF)
    inner = part_ref[...] - STEP_GAIN * dot(turned, rim_ref[...])
    side_columns(inner, kernels_ref, ext_ref[pl.ds(first, EXT), :], inv_side_ref, narrow_ref, held_ref, bands_ref)


def resist_of(blurred):
    return 0.5 * jnp.tanh((0.5 * STEEPNESS) * (blurred - THRESHOLD)) + 0.5


def stacked(low):
    stack = jnp.concatenate([low[:, 128 * g : 128 * (g + 1)] for g in range(USED)], 0)
    return jnp.concatenate([stack, stack], 1)


def blur_rows(cells, up, down, step, down_ref):
    segment = lax.axis_index("segment")
    width = cells.shape[1]
    top, center, bottom = cells[:RB], cells[RB : RB + ROWS], cells[RB + ROWS :]
    top = jnp.where(segment == 0, pltpu.roll(top, step, 1) * up, top)
    bottom = jnp.where(
        segment == lax.axis_size("segment") - 1, pltpu.roll(bottom, width - step, 1) * down, bottom
    )
    both = dot(down_ref[...], jnp.concatenate([top, center, bottom], 0).astype(BF))
    return both[:ROWS] + both[ROWS:]


def at_sides(narrow, g):
    part = narrow[:, 128 * (g // 8) : 128 * (g // 8) + 128]
    first = 2 * RB * (g % 8)
    return pltpu.roll(part, (128 - first) % 128, 1), pltpu.roll(part, (112 - first) % 128, 1)


def local_kernel(mine_ref, mine_side_ref, held_ref, inv_ref, slot_ref, down_ref, across_ref, mask_ref, target_ref,
                 inner_ref, once_ref, cells_ref):
    fine = dot(stacked(mine_ref[...]), across_ref[...])
    lane = lax.broadcasted_iota(jnp.int32, (1, 128), 1)
    mine_side = mine_side_ref[...]
    for g in range(SLOTS):
        if g < USED:
            left, right = at_sides(mine_side, g)
            part = fine[ROWS * g : ROWS * (g + 1)]
            left = jnp.where(lane < RB, left, part[:, :128])
            right = jnp.where(lane >= 128 - RB, right, part[:, 128:])
            part = jnp.concatenate([left, right], 1)
        else:
            part = jnp.zeros((ROWS, EDGE), F32)
        step = STEP_GAIN * (target_ref[g].astype(F32) - resist_of(part))
        once_ref[g] = (mask_ref[g].astype(F32) + step).astype(BF)
    for j in range(GROUPS):
        cells_ref[:, 512 * j : 512 * (j + 1)] = coarse_group(held_ref, j, EXT, inv_ref, slot_ref)
    low = blur_rows(cells_ref[...], slot_ref[1:2, :], slot_ref[2:3, :], 128, down_ref)
    inner_ref[...] = dot(stacked(low.astype(BF)), across_ref[...])


def final_kernel(inner_ref, near_ref, far_ref, pick_ref, narrow_ref, down_ref, once_ref, target_ref,
                 mask_hbm, resist_hbm, mask_ref, resist_ref, sems):
    def sent(n):
        four = pl.ds(4 * n, 4)
        return [
            pltpu.make_async_copy(resist_ref.at[four], resist_hbm.at[four], sems.at[n]),
            pltpu.make_async_copy(mask_ref.at[four], mask_hbm.at[four], sems.at[4 + n]),
        ]

    lane = lax.broadcasted_iota(jnp.int32, (1, 128), 1)
    for n in (3, 0, 1, 2):
        if n == 0:
            narrow = blur_rows(lent(near_ref, far_ref, pick_ref), narrow_ref[0:1, :256],
                               narrow_ref[1:2, :256], 2 * RB, down_ref)
        for g in range(4 * n, 4 * n + 4):
            if g < USED:
                left, right = at_sides(narrow, g)
                left = jnp.where(lane < RB, left, 0.0)
                right = jnp.where(lane >= 128 - RB, right, 0.0)
                part = inner_ref[ROWS * g : ROWS * (g + 1), :] + jnp.concatenate([left, right], 1)
            else:
                part = jnp.zeros((ROWS, EDGE), F32)
            part = resist_of(part)
            resist_ref[g] = part
            mask_ref[g] = (once_ref[g].astype(F32) + STEP_GAIN * (target_ref[g].astype(F32) - part)).astype(BF)
        for copy in sent(n):
            copy.start()
    for n in range(4):
        for copy in sent(n):
            copy.wait()


VMEM = pl.BlockSpec(memory_space=pltpu.VMEM)
SMEM = pl.BlockSpec(memory_space=pltpu.SMEM)
HBM = pl.BlockSpec(memory_space=pltpu.HBM)


def call(kernel, ins, outs, flops, scratch=(), name=None, place=VMEM, grant=32 * 2**20):
    size = sum(math.prod(o.shape) * o.dtype.itemsize for o in outs)
    return pl.pallas_call(
        kernel,
        out_shape=tuple(outs),
        in_specs=list(ins),
        out_specs=tuple(place for _ in outs),
        scratch_shapes=list(scratch),
        compiler_params=pltpu.CompilerParams(vmem_limit_bytes=grant),
        cost_estimate=pl.CostEstimate(flops=flops, bytes_accessed=2 * size, transcendentals=0),
        name=name,
    )


def swapped(block, first):
    pairs = [(i, i + 1) for i in range(first, lax.axis_size("tile") - 1, 2)]
    return lax.ppermute(block, "tile", pairs + [(j, i) for i, j in pairs])


def body(mask, target, spectra, dose, slot_row, side_source):
    t = {name: jnp.asarray(value) for name, value in tables().items()}
    shape = jax.ShapeDtypeStruct
    tile_rows = pltpu.VMEM((USED, ROWS, EDGE), BF)
    plane = spectra.transpose(0, 2, 1, 3).reshape(NK * KF * 2, KF)
    (y,) = call(
        start_kernel,
        [HBM] * 3,
        [shape((ROWS, 128 * USED), BF)],
        10**8,
        [tile_rows, tile_rows, pltpu.VMEM((EDGE, 256), BF), pltpu.SemaphoreType.DMA((3,))],
        name="start",
        grant=62 * 2**20,
    )(mask, target, t["cols"])
    rows_all = lax.all_gather(y, "segment", axis=0, tiled=True)
    held, bands, base, kernels, slot, narrow = call(
        first_kernel,
        [VMEM] * 5 + [SMEM] * 2,
        [
            shape((GROUPS, NK * COARSE, 256), BF),
            shape((COARSE, 256), BF),
            shape((64, 64 * USED), F32),
            shape((NK, 2, 32, 128), F32),
            shape((8, 128 * USED), F32),
            shape((8, 128 * GROUPS), F32),
        ],
        10**9,
        name="first",
    )(rows_all, t["rows"], plane, t["grid"], t["inv_side"], dose, slot_row)
    from_near = swapped(bands, 0)
    from_far = swapped(bands, 1)
    part, edge, mine, pick = call(
        inside_kernel,
        [VMEM] * 10 + [SMEM],
        [
            shape((64, 64 * USED), F32),
            shape((COARSE, 256), F32),
            shape((ROWS, 128 * USED), BF),
            shape((512, 256), BF),
        ],
        10**9,
        [
            pltpu.VMEM((COARSE, 128 * USED), F32),
            pltpu.VMEM((EDGE, 128 * USED), BF),
            pltpu.VMEM((64 * USED, EDGE), BF),
        ],
        name="inside",
    )(held, t["inv"], slot, t["tall"], t["across"], t["rows"], t["inside"], base, t["own"], t["reach"], side_source.T)
    held, bands, mine_side = call(
        second_kernel,
        [VMEM] * 12,
        [shape((GROUPS, NK * EXT, 256), BF), shape((EXT, 256), BF), shape((ROWS, 256), F32)],
        10**9,
        [pltpu.VMEM((EDGE, 256), F32)],
        name="second",
    )(from_near, from_far, pick, edge, narrow, t["tall"], t["rows"], t["rim"], part, kernels, t["ext"], t["inv_side"])
    from_near = swapped(bands, 0)
    from_far = swapped(bands, 1)
    inner, once = call(
        local_kernel,
        [VMEM] * 9,
        [shape((USED * ROWS, EDGE), F32), shape((SLOTS, ROWS, EDGE), BF)],
        10**9,
        [pltpu.VMEM((EXT, 128 * USED), F32)],
        name="local",
    )(mine, mine_side, held, t["inv"], slot, t["down"], t["across"], mask, target)
    return call(
        final_kernel,
        [VMEM] * 8,
        [shape((SLOTS, ROWS, EDGE), BF), shape((SLOTS, ROWS, EDGE), F32)],
        10**8,
        [
            pltpu.VMEM((SLOTS, ROWS, EDGE), BF),
            pltpu.VMEM((SLOTS, ROWS, EDGE), F32),
            pltpu.SemaphoreType.DMA((8,)),
        ],
        name="final",
        place=HBM,
    )(inner, from_near, from_far, pick, narrow, t["down"], once, target)


def solution(mesh):
    in_specs = (
        P("tile", "segment", None),
        P("tile", "segment", None),
        P(),
        P("tile"),
        P("tile"),
        P("tile", None),
    )
    out_specs = (P("tile", "segment", None), P("tile", "segment", None))
    return jax.shard_map(body, mesh=mesh, in_specs=in_specs, out_specs=out_specs, check_vma=False)
```

```python
import functools
import math

import jax
import jax.numpy as jnp
import ml_dtypes
import numpy as np
from jax import lax
from jax.experimental import pallas as pl
from jax.experimental.pallas import tpu as pltpu
from jax.sharding import PartitionSpec as P

EDGE = 256
KF = 31
NK = 12
RB = 8
SLOTS = 16
USED = 12
GROUPS = USED // 4
ROWS = 16
EXT = ROWS + 2 * RB
COARSE = 64
STEEPNESS = 1.5
THRESHOLD = 2.0
STEP_GAIN = 0.5
BF = jnp.bfloat16
F32 = jnp.float32


def bf16(x):
    return np.asarray(x, np.float32).astype(ml_dtypes.bfloat16)


def high_low(x):
    high = bf16(x)
    return high, bf16(np.asarray(x, np.float32) - high.astype(np.float32))


@functools.cache
def tables():
    freq = np.arange(32) - KF // 2
    live = (np.arange(32) < KF).astype(np.float64)

    def waves(position):
        angle = 2.0 * np.pi * ((np.asarray(position)[:, None] * freq[None, :]) % EDGE) / EDGE
        return np.cos(angle) * live, np.sin(angle) * live

    cos, sin = waves(np.arange(EDGE))
    t = {}
    t["cols"] = bf16(np.concatenate([np.tile(cos, (1, 4)), np.tile(-sin, (1, 4))], 1) / 16.0)
    t["rows"] = bf16(np.concatenate([cos, sin], 1).T / 16.0)
    ext_cos, ext_sin = waves((np.arange(EDGE + 2 * RB) - RB) % EDGE)
    t["ext"] = bf16(np.concatenate([ext_cos, ext_sin], 1))
    c_cos, c_sin = waves(np.arange(COARSE) * (EDGE // COARSE))
    t["grid"] = bf16(np.concatenate([c_cos, c_sin], 1))
    inv = np.zeros((256, 512))
    for i in range(4):
        r, c = slice(32 * i, 32 * i + 32), 128 * i
        inv[r, c : c + 64] = c_cos.T
        inv[r, c + 64 : c + 128] = c_sin.T
        r = slice(128 + 32 * i, 128 + 32 * i + 32)
        inv[r, c : c + 64] = -c_sin.T
        inv[r, c + 64 : c + 128] = c_cos.T
    t["inv"] = bf16(inv)
    d = np.arange(EDGE)[None, :] - (EDGE // COARSE) * np.arange(COARSE)[:, None]
    interp = np.ones((COARSE, EDGE))
    for m in range(1, 32):
        interp += 2.0 * np.cos(2.0 * np.pi * m * d / EDGE)
    interp /= COARSE
    taps = np.exp(-(np.arange(-RB, RB + 1.0) ** 2) / (2.0 * (RB / 2.0) ** 2))
    taps /= taps.sum()
    blur = np.zeros((EDGE, EDGE))
    above = np.zeros((EDGE, EDGE))
    below = np.zeros((EDGE, EDGE))
    for b in range(EDGE):
        for step in range(-RB, RB + 1):
            a = b + step
            (above if a < 0 else below if a >= EDGE else blur)[a % EDGE, b] += taps[step + RB]
    wide = np.concatenate([interp @ blur] * 2, 0)
    t["across"] = np.concatenate(high_low(wide), 0)
    side = np.concatenate([np.arange(RB), np.arange(EDGE - RB, EDGE)])
    own = np.zeros((128 * USED, 256))
    for g in range(USED):
        own[128 * g : 128 * (g + 1), 16 * g : 16 * (g + 1)] = wide[:, side]
    t["own"] = bf16(own)
    inside = np.zeros((4 * EDGE, 256))
    for i in range(4):
        r, c = slice(EDGE * i, EDGE * (i + 1)), 32 * i
        inside[r, c : c + 32] = cos / 16.0
        inside[r, 128 + c : 128 + c + 32] = -sin / 16.0
        inside[EDGE * i + side] = 0.0
    t["inside"] = bf16(inside)
    rim = np.zeros((256, 768))
    for g in range(USED):
        rim[16 * g : 16 * (g + 1), 32 * g : 32 * g + 32] = cos[side] / 16.0
        rim[16 * g : 16 * (g + 1), 384 + 32 * g : 384 + 32 * g + 32] = -sin[side] / 16.0
    t["rim"] = bf16(rim)
    e_cos, e_sin = waves(side)
    inv_side = np.zeros((256, 128))
    for i in range(4):
        r, c = slice(32 * i, 32 * i + 32), 32 * i
        inv_side[r, c : c + 16] = e_cos.T
        inv_side[r, c + 16 : c + 32] = e_sin.T
        r = slice(128 + 32 * i, 128 + 32 * i + 32)
        inv_side[r, c : c + 16] = -e_sin.T
        inv_side[r, c + 16 : c + 32] = e_cos.T
    t["inv_side"] = bf16(inv_side)
    reach = np.zeros((512, 256))
    for n in range(512):
        q = n % 16
        if n % 256 >= 128 + 128 or (n % 256 >= 128 and (n // 16) % 2):
            continue
        for p in range(16):
            if n < 256 and q >= 8 and p < 8:
                reach[n, p::16] = above[EDGE - RB + q - 8, p]
            if n >= 256 and q < 8 and p >= 8:
                reach[n, p::16] = below[q, EDGE - RB + p - 8]
    t["reach"] = bf16(reach)
    main_high, main_low = high_low((interp @ blur).T)
    t["tall"] = np.concatenate(
        [main_high, bf16((interp @ above).T), bf16((interp @ below).T), main_low], 1
    )
    down = np.zeros((ROWS, EXT))
    for r in range(ROWS):
        down[r, r : r + 2 * RB + 1] = taps
    t["down"] = np.concatenate(high_low(down), 0)
    return t


def dot(a, b):
    return jnp.dot(a, b, preferred_element_type=F32)


def lane_block(width, size):
    return lax.broadcasted_iota(jnp.int32, (1, width), 1) // size


def four_slots(blocks, place):
    total = blocks[0]
    for i in range(1, 4):
        total = jnp.where(place == i, blocks[i], total)
    return total


def start_kernel(mask_hbm, target_hbm, cols_hbm, y_ref, mask_ref, target_ref, cols_ref, sems):
    copies = [
        pltpu.make_async_copy(mask_hbm.at[pl.ds(0, USED)], mask_ref, sems.at[0]),
        pltpu.make_async_copy(cols_hbm, cols_ref, sems.at[1]),
        pltpu.make_async_copy(target_hbm.at[pl.ds(0, USED)], target_ref, sems.at[2]),
    ]
    for copy in copies:
        copy.start()
    for copy in copies:
        copy.wait()
    of_mask = dot(mask_ref[...].reshape(USED * ROWS, EDGE), cols_ref[...])
    of_target = dot(target_ref[...].reshape(USED * ROWS, EDGE), cols_ref[...])
    place = lane_block(256, 32) % 4
    for n, both in enumerate((of_mask, of_mask + STEP_GAIN * of_target)):
        for j in range(GROUPS):
            firsts = [(4 * j + i) * ROWS for i in range(4)]
            total = four_slots([both[f : f + ROWS] for f in firsts], place).astype(BF)
            lane = 768 * n + 128 * j
            y_ref[:, lane : lane + 128] = total[:, :128]
            y_ref[:, lane + 384 : lane + 512] = total[:, 128:]


def lay_kernels(plane_ref, kernels_ref):
    kernels_ref[...] = jnp.zeros_like(kernels_ref)
    for k in range(NK):
        for part in range(2):
            kernels_ref[k, part, :KF, :KF] = plane_ref[pl.ds(2 * KF * k + part, KF, stride=2), :]
    for k in range(NK):
        for part in range(2):
            one = kernels_ref[k, part]
            one = one + pltpu.roll(one, 32, 1)
            kernels_ref[k, part] = one + pltpu.roll(one, 64, 1)


def lay_slots(dose_ref, row_ref, slot_ref, narrow_ref):
    wide, narrow, quarter = lane_block(128 * USED, 128), lane_block(256, 2 * RB), lane_block(128 * GROUPS, 32)
    weight, up, down = (jnp.zeros((1, 128 * USED), F32) for _ in range(3))
    up_narrow, down_narrow = (jnp.zeros((1, 256), F32) for _ in range(2))
    weight_quarter = jnp.zeros((1, 128 * GROUPS), F32)
    for g in range(USED):
        row = row_ref[g]
        scale = jnp.where(row >= 0, dose_ref[g], 0.0) * (1.0 / (NK * KF * KF))
        weight = jnp.where(wide == g, scale, weight)
        weight_quarter = jnp.where(quarter == g, scale, weight_quarter)
        if g > 0:
            before = row_ref[g - 1]
            joined = jnp.where((before >= 0) & (row >= 0) & (before == row - 1), 1.0, 0.0)
            up = jnp.where(wide == g, joined, up)
            down = jnp.where(wide == g - 1, joined, down)
            up_narrow = jnp.where(narrow == g, joined, up_narrow)
            down_narrow = jnp.where(narrow == g - 1, joined, down_narrow)
    slot_ref[...] = jnp.concatenate([weight, up, down, jnp.zeros((5, 128 * USED), F32)], 0)
    narrow_ref[...] = jnp.concatenate(
        [
            jnp.concatenate([up_narrow, jnp.zeros((1, 128), F32)], 1),
            jnp.concatenate([down_narrow, jnp.zeros((1, 128), F32)], 1),
            weight_quarter,
            jnp.zeros((5, 128 * GROUPS), F32),
        ],
        0,
    )


def lay_pick(side_ref, reach_ref, pick_ref):
    narrow = lane_block(256, 2 * RB)
    row = lax.broadcasted_iota(jnp.int32, (256, 1), 0)
    source = jnp.where(row < 128, row // 32 + 4 * ((row // 16) % 2), 8 + (row - 128) // 32)
    for n in range(2):
        wanted = jnp.full((1, 256), -1, jnp.int32)
        for g in range(USED):
            wanted = jnp.where(narrow == g, side_ref[n, g], wanted)
        rows = slice(256 * n, 256 * (n + 1))
        pick_ref[rows, :] = jnp.where(source == wanted, reach_ref[rows, :].astype(F32), 0.0).astype(BF)


def side_columns(inner, kernels_ref, points, inv_side_ref, narrow_ref, held, bands_ref):
    count = points.shape[0]
    half = 32 * USED
    sides = []
    for j in range(GROUPS):
        lanes, more = slice(128 * j, 128 * (j + 1)), slice(half + 128 * j, half + 128 * (j + 1))
        re = inner[:32, lanes] + inner[32:, more]
        im = inner[:32, more] - inner[32:, lanes]
        for k in range(NK):
            k_re, k_im = kernels_ref[k, 0], kernels_ref[k, 1]
            p_re = k_re * re - k_im * im
            p_im = k_re * im + k_im * re
            block = jnp.concatenate(
                [jnp.concatenate([p_re, p_im], 1), jnp.concatenate([-p_im, p_re], 1)], 0
            ).astype(BF)
            held[j, k * count : (k + 1) * count, :] = dot(points, block).astype(BF)
        field = dot(held[j], inv_side_ref[...])
        squares = jnp.sum((field * field).reshape(NK, count, 128), axis=0)
        sides.append((squares + pltpu.roll(squares, 112, 1)) * narrow_ref[2:3, lanes])
    even = lane_block(128, 16) % 2 == 0
    bands_ref[:, :128] = jnp.where(even, sides[0], pltpu.roll(sides[1], 16, 1)).astype(BF)
    bands_ref[:, 128:] = jnp.where(even, sides[2], 0.0).astype(BF)


def coarse_group(held, j, count, inv_ref, slot_ref):
    field = dot(held[j], inv_ref[...])
    squares = jnp.sum((field * field).reshape(NK, count, 512), axis=0)
    return squares * slot_ref[0:1, 512 * j : 512 * (j + 1)]


def first_kernel(all_ref, rows_ref, plane_ref, grid_ref, inv_side_ref, dose_ref, row_ref,
                 held_ref, bands_ref, kernels_ref, slot_ref, narrow_ref):
    lay_kernels(plane_ref, kernels_ref)
    lay_slots(dose_ref, row_ref, slot_ref, narrow_ref)
    inner = dot(rows_ref[...], all_ref[:, :768])
    side_columns(inner, kernels_ref, grid_ref[...], inv_side_ref, narrow_ref, held_ref, bands_ref)


def inside_kernel(held_ref, inv_ref, slot_ref, tall_ref, across_ref, rows_ref, inside_ref, all_ref, own_ref,
                  reach_ref, side_ref, part_ref, edge_ref, mine_ref, pick_ref, cells_ref, blurred, resist_ref):
    lay_pick(side_ref, reach_ref, pick_ref)
    for j in range(GROUPS):
        cells_ref[:, 512 * j : 512 * (j + 1)] = coarse_group(held_ref, j, COARSE, inv_ref, slot_ref)
    cells = cells_ref[...]
    lanes = 128 * USED
    above = jnp.concatenate([cells[:, lanes - 128 :], cells[:, : lanes - 128]], 1) * slot_ref[1:2, :]
    below = jnp.concatenate([cells[:, 128:], cells[:, :128]], 1) * slot_ref[2:3, :]
    main = cells.astype(BF)
    edge_ref[...] = dot(main, own_ref[...])
    blurred[...] = dot(tall_ref[...], jnp.concatenate([main, above.astype(BF), below.astype(BF), main], 0)).astype(BF)
    first = pl.multiple_of(lax.axis_index("segment") * ROWS, ROWS)
    mine_ref[...] = blurred[pl.ds(first, ROWS), :]
    for g in range(USED):
        one = blurred[:, 128 * g : 128 * (g + 1)]
        fine = dot(jnp.concatenate([one, one], 1), across_ref[...])
        resist_ref[:, EDGE * g : EDGE * (g + 1)] = resist_of(fine).astype(BF)
    half = 32 * USED
    for j in range(GROUPS):
        change = dot(resist_ref[:, 4 * EDGE * j : 4 * EDGE * (j + 1)], inside_ref[...])
        firsts = (128 * j, half + 128 * j)
        before = jnp.concatenate([all_ref[:, 768 + f : 896 + f] for f in firsts], 1)
        y_part = (before.astype(F32) - STEP_GAIN * change).astype(BF)
        total = dot(rows_ref[...], y_part)
        for n, f in enumerate(firsts):
            part_ref[:, f : f + 128] = total[:, 128 * n : 128 * (n + 1)]


def lent(near_ref, far_ref, pick_ref):
    odd = lax.axis_index("tile") % 2 == 1
    far, near = far_ref[...].astype(F32), near_ref[...].astype(F32)
    left, right = jnp.where(odd, near, far), jnp.where(odd, far, near)
    return dot(jnp.concatenate([left, right], 1).astype(BF), pick_ref[...])


def second_kernel(near_ref, far_ref, pick_ref, edge_ref, narrow_ref, tall_ref, rows_ref, rim_ref, part_ref,
                  kernels_ref, ext_ref, inv_side_ref, held_ref, bands_ref, mine_side_ref, blurred):
    cells = edge_ref[...] + lent(near_ref, far_ref, pick_ref)
    above = pltpu.roll(cells, 2 * RB, 1) * narrow_ref[0:1, :256]
    below = pltpu.roll(cells, 256 - 2 * RB, 1) * narrow_ref[1:2, :256]
    main = cells.astype(BF)
    fine = dot(tall_ref[...], jnp.concatenate([main, above.astype(BF), below.astype(BF), main], 0))
    blurred[...] = fine
    first = pl.multiple_of(lax.axis_index("segment") * ROWS, ROWS)
    mine_side_ref[...] = blurred[pl.ds(first, ROWS), :]
    turned = dot(rows_ref[...], resist_of(fine).astype(BF)).astype(BF)
    inner = part_ref[...] - STEP_GAIN * dot(turned, rim_ref[...])
    side_columns(inner, kernels_ref, ext_ref[pl.ds(first, EXT), :], inv_side_ref, narrow_ref, held_ref, bands_ref)


def resist_of(blurred):
    return 0.5 * jnp.tanh((0.5 * STEEPNESS) * (blurred - THRESHOLD)) + 0.5


def stacked(low):
    stack = jnp.concatenate([low[:, 128 * g : 128 * (g + 1)] for g in range(USED)], 0)
    return jnp.concatenate([stack, stack], 1)


def blur_rows(cells, up, down, step, down_ref):
    segment = lax.axis_index("segment")
    width = cells.shape[1]
    top, center, bottom = cells[:RB], cells[RB : RB + ROWS], cells[RB + ROWS :]
    top = jnp.where(segment == 0, pltpu.roll(top, step, 1) * up, top)
    bottom = jnp.where(
        segment == lax.axis_size("segment") - 1, pltpu.roll(bottom, width - step, 1) * down, bottom
    )
    both = dot(down_ref[...], jnp.concatenate([top, center, bottom], 0).astype(BF))
    return both[:ROWS] + both[ROWS:]


def at_sides(narrow, g):
    part = narrow[:, 128 * (g // 8) : 128 * (g // 8) + 128]
    first = 2 * RB * (g % 8)
    return pltpu.roll(part, (128 - first) % 128, 1), pltpu.roll(part, (112 - first) % 128, 1)


def local_kernel(mine_ref, mine_side_ref, held_ref, inv_ref, slot_ref, down_ref, across_ref, mask_ref, target_ref,
                 inner_ref, once_ref, cells_ref):
    fine = dot(stacked(mine_ref[...]), across_ref[...])
    lane = lax.broadcasted_iota(jnp.int32, (1, 128), 1)
    mine_side = mine_side_ref[...]
    for g in range(SLOTS):
        if g < USED:
            left, right = at_sides(mine_side, g)
            part = fine[ROWS * g : ROWS * (g + 1)]
            left = jnp.where(lane < RB, left, part[:, :128])
            right = jnp.where(lane >= 128 - RB, right, part[:, 128:])
            part = jnp.concatenate([left, right], 1)
        else:
            part = jnp.zeros((ROWS, EDGE), F32)
        step = STEP_GAIN * (target_ref[g].astype(F32) - resist_of(part))
        once_ref[g] = (mask_ref[g].astype(F32) + step).astype(BF)
    for j in range(GROUPS):
        cells_ref[:, 512 * j : 512 * (j + 1)] = coarse_group(held_ref, j, EXT, inv_ref, slot_ref)
    low = blur_rows(cells_ref[...], slot_ref[1:2, :], slot_ref[2:3, :], 128, down_ref)
    inner_ref[...] = dot(stacked(low.astype(BF)), across_ref[...])


def final_kernel(inner_ref, near_ref, far_ref, pick_ref, narrow_ref, down_ref, once_ref, target_ref,
                 mask_hbm, resist_hbm, mask_ref, resist_ref, sems):
    def sent(n):
        four = pl.ds(4 * n, 4)
        return [
            pltpu.make_async_copy(resist_ref.at[four], resist_hbm.at[four], sems.at[n]),
            pltpu.make_async_copy(mask_ref.at[four], mask_hbm.at[four], sems.at[4 + n]),
        ]

    lane = lax.broadcasted_iota(jnp.int32, (1, 128), 1)
    for n in (3, 0, 1, 2):
        if n == 0:
            narrow = blur_rows(lent(near_ref, far_ref, pick_ref), narrow_ref[0:1, :256],
                               narrow_ref[1:2, :256], 2 * RB, down_ref)
        for g in range(4 * n, 4 * n + 4):
            if g < USED:
                left, right = at_sides(narrow, g)
                left = jnp.where(lane < RB, left, 0.0)
                right = jnp.where(lane >= 128 - RB, right, 0.0)
                part = inner_ref[ROWS * g : ROWS * (g + 1), :] + jnp.concatenate([left, right], 1)
            else:
                part = jnp.zeros((ROWS, EDGE), F32)
            part = resist_of(part)
            resist_ref[g] = part
            mask_ref[g] = (once_ref[g].astype(F32) + STEP_GAIN * (target_ref[g].astype(F32) - part)).astype(BF)
        for copy in sent(n):
            copy.start()
    for n in range(4):
        for copy in sent(n):
            copy.wait()


VMEM = pl.BlockSpec(memory_space=pltpu.VMEM)
SMEM = pl.BlockSpec(memory_space=pltpu.SMEM)
HBM = pl.BlockSpec(memory_space=pltpu.HBM)


def call(kernel, ins, outs, flops, scratch=(), name=None, place=VMEM, grant=32 * 2**20):
    size = sum(math.prod(o.shape) * o.dtype.itemsize for o in outs)
    return pl.pallas_call(
        kernel,
        out_shape=tuple(outs),
        in_specs=list(ins),
        out_specs=tuple(place for _ in outs),
        scratch_shapes=list(scratch),
        compiler_params=pltpu.CompilerParams(vmem_limit_bytes=grant),
        cost_estimate=pl.CostEstimate(flops=flops, bytes_accessed=2 * size, transcendentals=0),
        name=name,
    )


def swapped(block, first):
    pairs = [(i, i + 1) for i in range(first, lax.axis_size("tile") - 1, 2)]
    return lax.ppermute(block, "tile", pairs + [(j, i) for i, j in pairs])


def body(mask, target, spectra, dose, slot_row, side_source):
    t = {name: jnp.asarray(value) for name, value in tables().items()}
    shape = jax.ShapeDtypeStruct
    tile_rows = pltpu.VMEM((USED, ROWS, EDGE), BF)
    plane = spectra.transpose(0, 2, 1, 3).reshape(NK * KF * 2, KF)
    (y,) = call(
        start_kernel,
        [HBM] * 3,
        [shape((ROWS, 128 * USED), BF)],
        10**8,
        [tile_rows, tile_rows, pltpu.VMEM((EDGE, 256), BF), pltpu.SemaphoreType.DMA((3,))],
        name="start",
        grant=62 * 2**20,
    )(mask, target, t["cols"])
    rows_all = lax.all_gather(y, "segment", axis=0, tiled=True)
    held, bands, kernels, slot, narrow = call(
        first_kernel,
        [VMEM] * 5 + [SMEM] * 2,
        [
            shape((GROUPS, NK * COARSE, 256), BF),
            shape((COARSE, 256), BF),
            shape((NK, 2, 32, 128), F32),
            shape((8, 128 * USED), F32),
            shape((8, 128 * GROUPS), F32),
        ],
        10**9,
        name="first",
    )(rows_all, t["rows"], plane, t["grid"], t["inv_side"], dose, slot_row)
    from_near = swapped(bands, 0)
    from_far = swapped(bands, 1)
    part, edge, mine, pick = call(
        inside_kernel,
        [VMEM] * 10 + [SMEM],
        [
            shape((64, 64 * USED), F32),
            shape((COARSE, 256), F32),
            shape((ROWS, 128 * USED), BF),
            shape((512, 256), BF),
        ],
        10**9,
        [
            pltpu.VMEM((COARSE, 128 * USED), F32),
            pltpu.VMEM((EDGE, 128 * USED), BF),
            pltpu.VMEM((EDGE, EDGE * USED), BF),
        ],
        name="inside",
    )(held, t["inv"], slot, t["tall"], t["across"], t["rows"], t["inside"], rows_all, t["own"], t["reach"], side_source.T)
    held, bands, mine_side = call(
        second_kernel,
        [VMEM] * 12,
        [shape((GROUPS, NK * EXT, 256), BF), shape((EXT, 256), BF), shape((ROWS, 256), F32)],
        10**9,
        [pltpu.VMEM((EDGE, 256), F32)],
        name="second",
    )(from_near, from_far, pick, edge, narrow, t["tall"], t["rows"], t["rim"], part, kernels, t["ext"], t["inv_side"])
    from_near = swapped(bands, 0)
    from_far = swapped(bands, 1)
    inner, once = call(
        local_kernel,
        [VMEM] * 9,
        [shape((USED * ROWS, EDGE), F32), shape((SLOTS, ROWS, EDGE), BF)],
        10**9,
        [pltpu.VMEM((EXT, 128 * USED), F32)],
        name="local",
    )(mine, mine_side, held, t["inv"], slot, t["down"], t["across"], mask, target)
    return call(
        final_kernel,
        [VMEM] * 8,
        [shape((SLOTS, ROWS, EDGE), BF), shape((SLOTS, ROWS, EDGE), F32)],
        10**8,
        [
            pltpu.VMEM((SLOTS, ROWS, EDGE), BF),
            pltpu.VMEM((SLOTS, ROWS, EDGE), F32),
            pltpu.SemaphoreType.DMA((8,)),
        ],
        name="final",
        place=HBM,
    )(inner, from_near, from_far, pick, narrow, t["down"], once, target)


def solution(mesh):
    in_specs = (
        P("tile", "segment", None),
        P("tile", "segment", None),
        P(),
        P("tile"),
        P("tile"),
        P("tile", None),
    )
    out_specs = (P("tile", "segment", None), P("tile", "segment", None))
    return jax.shard_map(body, mesh=mesh, in_specs=in_specs, out_specs=out_specs, check_vma=False)
```

```python
import functools
import math

import jax
import jax.numpy as jnp
import ml_dtypes
import numpy as np
from jax import lax
from jax.experimental import pallas as pl
from jax.experimental.pallas import tpu as pltpu
from jax.sharding import PartitionSpec as P

EDGE = 256
KF = 31
NK = 12
RB = 8
SLOTS = 16
USED = 12
GROUPS = USED // 4
ROWS = 16
EXT = ROWS + 2 * RB
COARSE = 64
STEEPNESS = 1.5
THRESHOLD = 2.0
STEP_GAIN = 0.5
BF = jnp.bfloat16
F32 = jnp.float32


def bf16(x):
    return np.asarray(x, np.float32).astype(ml_dtypes.bfloat16)


def high_low(x):
    high = bf16(x)
    return high, bf16(np.asarray(x, np.float32) - high.astype(np.float32))


@functools.cache
def tables():
    freq = np.arange(32) - KF // 2
    live = (np.arange(32) < KF).astype(np.float64)

    def waves(position):
        angle = 2.0 * np.pi * ((np.asarray(position)[:, None] * freq[None, :]) % EDGE) / EDGE
        return np.cos(angle) * live, np.sin(angle) * live

    cos, sin = waves(np.arange(EDGE))
    t = {}
    t["cols"] = bf16(np.concatenate([np.tile(cos, (1, 4)), np.tile(-sin, (1, 4))], 1) / 16.0)
    t["rows"] = bf16(np.concatenate([cos, sin], 1).T / 16.0)
    ext_cos, ext_sin = waves((np.arange(EDGE + 2 * RB) - RB) % EDGE)
    t["ext"] = bf16(np.concatenate([ext_cos, -ext_sin, ext_sin, ext_cos], 1))
    c_cos, c_sin = waves(np.arange(COARSE) * (EDGE // COARSE))
    t["grid"] = bf16(np.block([[c_cos, -c_sin], [c_sin, c_cos]]))
    inv = np.zeros((256, 512))
    for i in range(4):
        r, c = slice(32 * i, 32 * i + 32), 128 * i
        inv[r, c : c + 64] = c_cos.T
        inv[r, c + 64 : c + 128] = c_sin.T
        r = slice(128 + 32 * i, 128 + 32 * i + 32)
        inv[r, c : c + 64] = -c_sin.T
        inv[r, c + 64 : c + 128] = c_cos.T
    t["inv"] = bf16(inv)
    d = np.arange(EDGE)[None, :] - (EDGE // COARSE) * np.arange(COARSE)[:, None]
    interp = np.ones((COARSE, EDGE))
    for m in range(1, 32):
        interp += 2.0 * np.cos(2.0 * np.pi * m * d / EDGE)
    interp /= COARSE
    taps = np.exp(-(np.arange(-RB, RB + 1.0) ** 2) / (2.0 * (RB / 2.0) ** 2))
    taps /= taps.sum()
    blur = np.zeros((EDGE, EDGE))
    above = np.zeros((EDGE, EDGE))
    below = np.zeros((EDGE, EDGE))
    for b in range(EDGE):
        for step in range(-RB, RB + 1):
            a = b + step
            (above if a < 0 else below if a >= EDGE else blur)[a % EDGE, b] += taps[step + RB]
    wide = np.concatenate([interp @ blur] * 2, 0)
    t["across"] = np.concatenate(high_low(wide), 0)
    side = np.concatenate([np.arange(RB), np.arange(EDGE - RB, EDGE)])
    own = np.zeros((128 * USED, 256))
    for g in range(USED):
        own[128 * g : 128 * (g + 1), 16 * g : 16 * (g + 1)] = wide[:, side]
    t["own"] = bf16(own)
    inside = np.zeros((4 * EDGE, 256))
    for i in range(4):
        r, c = slice(EDGE * i, EDGE * (i + 1)), 32 * i
        inside[r, c : c + 32] = cos / 16.0
        inside[r, 128 + c : 128 + c + 32] = -sin / 16.0
        inside[EDGE * i + side] = 0.0
    t["inside"] = bf16(inside)
    rim = np.zeros((256, 768))
    for g in range(USED):
        rim[16 * g : 16 * (g + 1), 32 * g : 32 * g + 32] = cos[side] / 16.0
        rim[16 * g : 16 * (g + 1), 384 + 32 * g : 384 + 32 * g + 32] = -sin[side] / 16.0
    t["rim"] = bf16(rim)
    e_cos, e_sin = waves(side)
    inv_side = np.zeros((256, 128))
    for i in range(4):
        r, c = slice(32 * i, 32 * i + 32), 32 * i
        inv_side[r, c : c + 16] = e_cos.T
        inv_side[r, c + 16 : c + 32] = e_sin.T
        r = slice(128 + 32 * i, 128 + 32 * i + 32)
        inv_side[r, c : c + 16] = -e_sin.T
        inv_side[r, c + 16 : c + 32] = e_cos.T
    t["inv_side"] = bf16(inv_side)
    reach = np.zeros((512, 256))
    for n in range(512):
        q = n % 16
        if n % 256 >= 128 + 128 or (n % 256 >= 128 and (n // 16) % 2):
            continue
        for p in range(16):
            if n < 256 and q >= 8 and p < 8:
                reach[n, p::16] = above[EDGE - RB + q - 8, p]
            if n >= 256 and q < 8 and p >= 8:
                reach[n, p::16] = below[q, EDGE - RB + p - 8]
    t["reach"] = bf16(reach)
    main_high, main_low = high_low((interp @ blur).T)
    t["tall"] = np.concatenate(
        [main_high, bf16((interp @ above).T), bf16((interp @ below).T), main_low], 1
    )
    down = np.zeros((ROWS, EXT))
    for r in range(ROWS):
        down[r, r : r + 2 * RB + 1] = taps
    t["down"] = np.concatenate(high_low(down), 0)
    return t


def dot(a, b):
    return jnp.dot(a, b, preferred_element_type=F32)


def lane_block(width, size):
    return lax.broadcasted_iota(jnp.int32, (1, width), 1) // size


def four_slots(blocks, place):
    total = blocks[0]
    for i in range(1, 4):
        total = jnp.where(place == i, blocks[i], total)
    return total


def start_kernel(mask_hbm, target_hbm, cols_hbm, y_ref, mask_ref, target_ref, cols_ref, sems):
    copies = [
        pltpu.make_async_copy(mask_hbm.at[pl.ds(0, USED)], mask_ref, sems.at[0]),
        pltpu.make_async_copy(cols_hbm, cols_ref, sems.at[1]),
        pltpu.make_async_copy(target_hbm.at[pl.ds(0, USED)], target_ref, sems.at[2]),
    ]
    for copy in copies:
        copy.start()
    copies[0].wait()
    copies[1].wait()
    of_mask = dot(mask_ref[...].reshape(USED * ROWS, EDGE), cols_ref[...])
    copies[2].wait()
    of_target = dot(target_ref[...].reshape(USED * ROWS, EDGE), cols_ref[...])
    place = lane_block(256, 32) % 4
    for n, both in enumerate((of_mask, of_mask + STEP_GAIN * of_target)):
        for j in range(GROUPS):
            firsts = [(4 * j + i) * ROWS for i in range(4)]
            total = four_slots([both[f : f + ROWS] for f in firsts], place).astype(BF)
            lane = 768 * n + 128 * j
            y_ref[:, lane : lane + 128] = total[:, :128]
            y_ref[:, lane + 384 : lane + 512] = total[:, 128:]


def lay_kernels(plane_ref, kernels_ref):
    kernels_ref[...] = jnp.zeros_like(kernels_ref)
    for k in range(NK):
        for part in range(2):
            kernels_ref[k, part, :KF, :KF] = plane_ref[pl.ds(2 * KF * k + part, KF, stride=2), :]
    for k in range(NK):
        for part in range(2):
            one = kernels_ref[k, part]
            one = one + pltpu.roll(one, 32, 1)
            kernels_ref[k, part] = one + pltpu.roll(one, 64, 1)


def lay_slots(dose_ref, row_ref, slot_ref, narrow_ref):
    wide, narrow, quarter = lane_block(128 * USED, 128), lane_block(256, 2 * RB), lane_block(128 * GROUPS, 32)
    weight, up, down = (jnp.zeros((1, 128 * USED), F32) for _ in range(3))
    up_narrow, down_narrow = (jnp.zeros((1, 256), F32) for _ in range(2))
    weight_quarter = jnp.zeros((1, 128 * GROUPS), F32)
    rows, doses = row_ref[...], dose_ref[...]
    for g in range(USED):
        row = rows[:, g : g + 1]
        scale = jnp.where(row >= 0, doses[:, g : g + 1], 0.0) * (1.0 / (NK * KF * KF))
        weight = jnp.where(wide == g, scale, weight)
        weight_quarter = jnp.where(quarter == g, scale, weight_quarter)
        if g > 0:
            before = rows[:, g - 1 : g]
            joined = jnp.where((before >= 0) & (row >= 0) & (before == row - 1), 1.0, 0.0)
            up = jnp.where(wide == g, joined, up)
            down = jnp.where(wide == g - 1, joined, down)
            up_narrow = jnp.where(narrow == g, joined, up_narrow)
            down_narrow = jnp.where(narrow == g - 1, joined, down_narrow)
    slot_ref[...] = jnp.concatenate([weight, up, down, jnp.zeros((5, 128 * USED), F32)], 0)
    narrow_ref[...] = jnp.concatenate(
        [
            jnp.concatenate([up_narrow, jnp.zeros((1, 128), F32)], 1),
            jnp.concatenate([down_narrow, jnp.zeros((1, 128), F32)], 1),
            weight_quarter,
            jnp.zeros((5, 128 * GROUPS), F32),
        ],
        0,
    )


def lay_pick(side_ref, reach_ref, pick_ref):
    narrow = lane_block(256, 2 * RB)
    row = lax.broadcasted_iota(jnp.int32, (256, 1), 0)
    source = jnp.where(row < 128, row // 32 + 4 * ((row // 16) % 2), 8 + (row - 128) // 32)
    sources = side_ref[...]
    for n in range(2):
        wanted = jnp.full((1, 256), -1, jnp.int32)
        for g in range(USED):
            wanted = jnp.where(narrow == g, sources[n : n + 1, g : g + 1], wanted)
        rows = slice(256 * n, 256 * (n + 1))
        pick_ref[rows, :] = jnp.where(source == wanted, reach_ref[rows, :].astype(F32), 0.0).astype(BF)


def side_columns(inner, kernels_ref, points, inv_side_ref, narrow_ref, held, bands_ref):
    count = points.shape[0] // 2
    half = 32 * USED
    sides = []
    for j in range(GROUPS):
        lanes, more = slice(128 * j, 128 * (j + 1)), slice(half + 128 * j, half + 128 * (j + 1))
        re = inner[:32, lanes] + inner[32:, more]
        im = inner[:32, more] - inner[32:, lanes]
        for k in range(0, NK, 2):
            pair = []
            for n in (k, k + 1):
                k_re, k_im = kernels_ref[n, 0], kernels_ref[n, 1]
                pair.append(jnp.concatenate([k_re * re - k_im * im, k_re * im + k_im * re], 0).astype(BF))
            both = dot(points, jnp.concatenate(pair, 1)).astype(BF)
            for n in range(2):
                rows, lane = slice((k + n) * count, (k + n + 1) * count), 128 * n
                held[j, rows, :128] = both[:count, lane : lane + 128]
                held[j, rows, 128:] = both[count:, lane : lane + 128]
        field = dot(held[j], inv_side_ref[...])
        squares = jnp.sum((field * field).reshape(NK, count, 128), axis=0)
        sides.append((squares + pltpu.roll(squares, 112, 1)) * narrow_ref[2:3, lanes])
    even = lane_block(128, 16) % 2 == 0
    bands_ref[:, :128] = jnp.where(even, sides[0], pltpu.roll(sides[1], 16, 1)).astype(BF)
    bands_ref[:, 128:] = jnp.where(even, sides[2], 0.0).astype(BF)


def coarse_group(held, j, count, inv_ref, slot_ref):
    field = dot(held[j], inv_ref[...])
    squares = jnp.sum((field * field).reshape(NK, count, 512), axis=0)
    return squares * slot_ref[0:1, 512 * j : 512 * (j + 1)]


def first_kernel(all_ref, rows_ref, plane_ref, grid_ref, inv_side_ref, dose_ref, row_ref,
                 held_ref, bands_ref, kernels_ref, slot_ref, narrow_ref):
    lay_kernels(plane_ref, kernels_ref)
    lay_slots(dose_ref, row_ref, slot_ref, narrow_ref)
    inner = dot(rows_ref[...], all_ref[:, :768])
    side_columns(inner, kernels_ref, grid_ref[...], inv_side_ref, narrow_ref, held_ref, bands_ref)


def inside_kernel(held_ref, inv_ref, slot_ref, tall_ref, across_ref, rows_ref, inside_ref, all_ref, own_ref,
                  reach_ref, side_ref, part_ref, edge_ref, mine_ref, pick_ref, cells_ref, blurred, resist_ref):
    lay_pick(side_ref, reach_ref, pick_ref)
    for j in range(GROUPS):
        cells_ref[:, 512 * j : 512 * (j + 1)] = coarse_group(held_ref, j, COARSE, inv_ref, slot_ref)
    cells = cells_ref[...]
    lanes = 128 * USED
    above = jnp.concatenate([cells[:, lanes - 128 :], cells[:, : lanes - 128]], 1) * slot_ref[1:2, :]
    below = jnp.concatenate([cells[:, 128:], cells[:, :128]], 1) * slot_ref[2:3, :]
    main = cells.astype(BF)
    edge_ref[...] = dot(main, own_ref[...])
    blurred[...] = dot(tall_ref[...], jnp.concatenate([main, above.astype(BF), below.astype(BF), main], 0)).astype(BF)
    first = pl.multiple_of(lax.axis_index("segment") * ROWS, ROWS)
    mine_ref[...] = blurred[pl.ds(first, ROWS), :]
    for g in range(USED):
        one = blurred[:, 128 * g : 128 * (g + 1)]
        fine = dot(jnp.concatenate([one, one], 1), across_ref[...])
        resist_ref[:, EDGE * g : EDGE * (g + 1)] = resist_of(fine).astype(BF)
    half = 32 * USED
    for j in range(GROUPS):
        change = dot(resist_ref[:, 4 * EDGE * j : 4 * EDGE * (j + 1)], inside_ref[...])
        firsts = (128 * j, half + 128 * j)
        before = jnp.concatenate([all_ref[:, 768 + f : 896 + f] for f in firsts], 1)
        y_part = (before.astype(F32) - STEP_GAIN * change).astype(BF)
        total = dot(rows_ref[...], y_part)
        for n, f in enumerate(firsts):
            part_ref[:, f : f + 128] = total[:, 128 * n : 128 * (n + 1)]


def lent(near_ref, far_ref, pick_ref):
    odd = lax.axis_index("tile") % 2 == 1
    far, near = far_ref[...].astype(F32), near_ref[...].astype(F32)
    left, right = jnp.where(odd, near, far), jnp.where(odd, far, near)
    return dot(jnp.concatenate([left, right], 1).astype(BF), pick_ref[...])


def second_kernel(near_ref, far_ref, pick_ref, edge_ref, narrow_ref, tall_ref, rows_ref, rim_ref, part_ref,
                  kernels_ref, ext_ref, inv_side_ref, held_ref, bands_ref, mine_side_ref, blurred):
    cells = edge_ref[...] + lent(near_ref, far_ref, pick_ref)
    above = pltpu.roll(cells, 2 * RB, 1) * narrow_ref[0:1, :256]
    below = pltpu.roll(cells, 256 - 2 * RB, 1) * narrow_ref[1:2, :256]
    main = cells.astype(BF)
    fine = dot(tall_ref[...], jnp.concatenate([main, above.astype(BF), below.astype(BF), main], 0))
    blurred[...] = fine
    first = pl.multiple_of(lax.axis_index("segment") * ROWS, ROWS)
    mine_side_ref[...] = blurred[pl.ds(first, ROWS), :]
    turned = dot(rows_ref[...], resist_of(fine).astype(BF)).astype(BF)
    inner = part_ref[...] - STEP_GAIN * dot(turned, rim_ref[...])
    ext = ext_ref[pl.ds(first, EXT), :]
    points = jnp.concatenate([ext[:, :64], ext[:, 64:]], 0)
    side_columns(inner, kernels_ref, points, inv_side_ref, narrow_ref, held_ref, bands_ref)


def resist_of(blurred):
    return 0.5 * jnp.tanh((0.5 * STEEPNESS) * (blurred - THRESHOLD)) + 0.5


def stacked(low):
    stack = jnp.concatenate([low[:, 128 * g : 128 * (g + 1)] for g in range(USED)], 0)
    return jnp.concatenate([stack, stack], 1)


def blur_rows(cells, up, down, step, down_ref):
    segment = lax.axis_index("segment")
    width = cells.shape[1]
    top, center, bottom = cells[:RB], cells[RB : RB + ROWS], cells[RB + ROWS :]
    top = jnp.where(segment == 0, pltpu.roll(top, step, 1) * up, top)
    bottom = jnp.where(
        segment == lax.axis_size("segment") - 1, pltpu.roll(bottom, width - step, 1) * down, bottom
    )
    both = dot(down_ref[...], jnp.concatenate([top, center, bottom], 0).astype(BF))
    return both[:ROWS] + both[ROWS:]


def at_sides(narrow, g):
    part = narrow[:, 128 * (g // 8) : 128 * (g // 8) + 128]
    first = 2 * RB * (g % 8)
    return pltpu.roll(part, (128 - first) % 128, 1), pltpu.roll(part, (112 - first) % 128, 1)


def local_kernel(mine_ref, mine_side_ref, held_ref, inv_ref, slot_ref, down_ref, across_ref, mask_ref, target_ref,
                 inner_ref, once_ref, cells_ref):
    fine = dot(stacked(mine_ref[...]), across_ref[...])
    lane = lax.broadcasted_iota(jnp.int32, (1, 128), 1)
    mine_side = mine_side_ref[...]
    for g in range(SLOTS):
        if g < USED:
            left, right = at_sides(mine_side, g)
            part = fine[ROWS * g : ROWS * (g + 1)]
            left = jnp.where(lane < RB, left, part[:, :128])
            right = jnp.where(lane >= 128 - RB, right, part[:, 128:])
            part = jnp.concatenate([left, right], 1)
        else:
            part = jnp.zeros((ROWS, EDGE), F32)
        step = STEP_GAIN * (target_ref[g].astype(F32) - resist_of(part))
        once_ref[g] = (mask_ref[g].astype(F32) + step).astype(BF)
    for j in range(GROUPS):
        cells_ref[:, 512 * j : 512 * (j + 1)] = coarse_group(held_ref, j, EXT, inv_ref, slot_ref)
    low = blur_rows(cells_ref[...], slot_ref[1:2, :], slot_ref[2:3, :], 128, down_ref)
    inner_ref[...] = dot(stacked(low.astype(BF)), across_ref[...])


def final_kernel(inner_ref, near_ref, far_ref, pick_ref, narrow_ref, down_ref, once_ref, target_ref,
                 mask_hbm, resist_hbm, mask_ref, resist_ref, sems):
    def sent(n):
        four = pl.ds(4 * n, 4)
        return [
            pltpu.make_async_copy(resist_ref.at[four], resist_hbm.at[four], sems.at[n]),
            pltpu.make_async_copy(mask_ref.at[four], mask_hbm.at[four], sems.at[4 + n]),
        ]

    lane = lax.broadcasted_iota(jnp.int32, (1, 128), 1)
    for n in (3, 0, 1, 2):
        if n == 0:
            narrow = blur_rows(lent(near_ref, far_ref, pick_ref), narrow_ref[0:1, :256],
                               narrow_ref[1:2, :256], 2 * RB, down_ref)
        for g in range(4 * n, 4 * n + 4):
            if g < USED:
                left, right = at_sides(narrow, g)
                left = jnp.where(lane < RB, left, 0.0)
                right = jnp.where(lane >= 128 - RB, right, 0.0)
                part = inner_ref[ROWS * g : ROWS * (g + 1), :] + jnp.concatenate([left, right], 1)
            else:
                part = jnp.zeros((ROWS, EDGE), F32)
            part = resist_of(part)
            resist_ref[g] = part
            mask_ref[g] = (once_ref[g].astype(F32) + STEP_GAIN * (target_ref[g].astype(F32) - part)).astype(BF)
        for copy in sent(n):
            copy.start()
    for n in range(4):
        for copy in sent(n):
            copy.wait()


VMEM = pl.BlockSpec(memory_space=pltpu.VMEM)
HBM = pl.BlockSpec(memory_space=pltpu.HBM)


def call(kernel, ins, outs, flops, scratch=(), name=None, place=VMEM, grant=32 * 2**20):
    size = sum(math.prod(o.shape) * o.dtype.itemsize for o in outs)
    return pl.pallas_call(
        kernel,
        out_shape=tuple(outs),
        in_specs=list(ins),
        out_specs=tuple(place for _ in outs),
        scratch_shapes=list(scratch),
        compiler_params=pltpu.CompilerParams(vmem_limit_bytes=grant),
        cost_estimate=pl.CostEstimate(flops=flops, bytes_accessed=2 * size, transcendentals=0),
        name=name,
    )


def swapped(block, first):
    pairs = [(i, i + 1) for i in range(first, lax.axis_size("tile") - 1, 2)]
    return lax.ppermute(block, "tile", pairs + [(j, i) for i, j in pairs])


def body(mask, target, spectra, dose, slot_row, side_source):
    t = {name: jnp.asarray(value) for name, value in tables().items()}
    shape = jax.ShapeDtypeStruct
    tile_rows = pltpu.VMEM((USED, ROWS, EDGE), BF)
    plane = spectra.transpose(0, 2, 1, 3).reshape(NK * KF * 2, KF)
    (y,) = call(
        start_kernel,
        [HBM] * 3,
        [shape((ROWS, 128 * USED), BF)],
        10**8,
        [tile_rows, tile_rows, pltpu.VMEM((EDGE, 256), BF), pltpu.SemaphoreType.DMA((3,))],
        name="start",
        grant=62 * 2**20,
    )(mask, target, t["cols"])
    rows_all = lax.all_gather(y, "segment", axis=0, tiled=True)
    held, bands, kernels, slot, narrow = call(
        first_kernel,
        [VMEM] * 7,
        [
            shape((GROUPS, NK * COARSE, 256), BF),
            shape((COARSE, 256), BF),
            shape((NK, 2, 32, 128), F32),
            shape((8, 128 * USED), F32),
            shape((8, 128 * GROUPS), F32),
        ],
        10**9,
        name="first",
    )(rows_all, t["rows"], plane, t["grid"], t["inv_side"], dose.reshape(1, SLOTS), slot_row.reshape(1, SLOTS))
    from_near = swapped(bands, 0)
    from_far = swapped(bands, 1)
    part, edge, mine, pick = call(
        inside_kernel,
        [VMEM] * 11,
        [
            shape((64, 64 * USED), F32),
            shape((COARSE, 256), F32),
            shape((ROWS, 128 * USED), BF),
            shape((512, 256), BF),
        ],
        10**9,
        [
            pltpu.VMEM((COARSE, 128 * USED), F32),
            pltpu.VMEM((EDGE, 128 * USED), BF),
            pltpu.VMEM((EDGE, EDGE * USED), BF),
        ],
        name="inside",
    )(held, t["inv"], slot, t["tall"], t["across"], t["rows"], t["inside"], rows_all, t["own"], t["reach"], side_source.T)
    held, bands, mine_side = call(
        second_kernel,
        [VMEM] * 12,
        [shape((GROUPS, NK * EXT, 256), BF), shape((EXT, 256), BF), shape((ROWS, 256), F32)],
        10**9,
        [pltpu.VMEM((EDGE, 256), F32)],
        name="second",
    )(from_near, from_far, pick, edge, narrow, t["tall"], t["rows"], t["rim"], part, kernels, t["ext"], t["inv_side"])
    from_near = swapped(bands, 0)
    from_far = swapped(bands, 1)
    inner, once = call(
        local_kernel,
        [VMEM] * 9,
        [shape((USED * ROWS, EDGE), F32), shape((SLOTS, ROWS, EDGE), BF)],
        10**9,
        [pltpu.VMEM((EXT, 128 * USED), F32)],
        name="local",
    )(mine, mine_side, held, t["inv"], slot, t["down"], t["across"], mask, target)
    return call(
        final_kernel,
        [VMEM] * 8,
        [shape((SLOTS, ROWS, EDGE), BF), shape((SLOTS, ROWS, EDGE), F32)],
        10**8,
        [
            pltpu.VMEM((SLOTS, ROWS, EDGE), BF),
            pltpu.VMEM((SLOTS, ROWS, EDGE), F32),
            pltpu.SemaphoreType.DMA((8,)),
        ],
        name="final",
        place=HBM,
    )(inner, from_near, from_far, pick, narrow, t["down"], once, target)


def solution(mesh):
    in_specs = (
        P("tile", "segment", None),
        P("tile", "segment", None),
        P(),
        P("tile"),
        P("tile"),
        P("tile", None),
    )
    out_specs = (P("tile", "segment", None), P("tile", "segment", None))
    return jax.shard_map(body, mesh=mesh, in_specs=in_specs, out_specs=out_specs, check_vma=False)
```

```python
import functools
import math

import jax
import jax.numpy as jnp
import ml_dtypes
import numpy as np
from jax import lax
from jax.experimental import pallas as pl
from jax.experimental.pallas import tpu as pltpu
from jax.sharding import PartitionSpec as P

EDGE = 256
KF = 31
NK = 12
RB = 8
SLOTS = 16
USED = 12
GROUPS = USED // 4
ROWS = 16
EXT = ROWS + 2 * RB
COARSE = 64
STEEPNESS = 1.5
THRESHOLD = 2.0
STEP_GAIN = 0.5
BF = jnp.bfloat16
F32 = jnp.float32


def bf16(x):
    return np.asarray(x, np.float32).astype(ml_dtypes.bfloat16)


def high_low(x):
    high = bf16(x)
    return high, bf16(np.asarray(x, np.float32) - high.astype(np.float32))


@functools.cache
def tables():
    freq = np.arange(32) - KF // 2
    live = (np.arange(32) < KF).astype(np.float64)

    def waves(position):
        angle = 2.0 * np.pi * ((np.asarray(position)[:, None] * freq[None, :]) % EDGE) / EDGE
        return np.cos(angle) * live, np.sin(angle) * live

    cos, sin = waves(np.arange(EDGE))
    t = {}
    t["cols"] = bf16(np.concatenate([np.tile(cos, (1, 4)), np.tile(-sin, (1, 4))], 1) / 16.0)
    t["rows"] = bf16(np.concatenate([cos, sin], 1).T / 16.0)
    ext_cos, ext_sin = waves((np.arange(EDGE + 2 * RB) - RB) % EDGE)
    t["ext"] = bf16(np.concatenate([ext_cos, -ext_sin, ext_sin, ext_cos], 1))
    c_cos, c_sin = waves(np.arange(COARSE) * (EDGE // COARSE))
    t["grid"] = bf16(np.block([[c_cos, -c_sin], [c_sin, c_cos]]))
    inv = np.zeros((256, 512))
    for i in range(4):
        r, c = slice(32 * i, 32 * i + 32), 128 * i
        inv[r, c : c + 64] = c_cos.T
        inv[r, c + 64 : c + 128] = c_sin.T
        r = slice(128 + 32 * i, 128 + 32 * i + 32)
        inv[r, c : c + 64] = -c_sin.T
        inv[r, c + 64 : c + 128] = c_cos.T
    t["inv"] = bf16(inv)
    d = np.arange(EDGE)[None, :] - (EDGE // COARSE) * np.arange(COARSE)[:, None]
    interp = np.ones((COARSE, EDGE))
    for m in range(1, 32):
        interp += 2.0 * np.cos(2.0 * np.pi * m * d / EDGE)
    interp /= COARSE
    taps = np.exp(-(np.arange(-RB, RB + 1.0) ** 2) / (2.0 * (RB / 2.0) ** 2))
    taps /= taps.sum()
    blur = np.zeros((EDGE, EDGE))
    above = np.zeros((EDGE, EDGE))
    below = np.zeros((EDGE, EDGE))
    for b in range(EDGE):
        for step in range(-RB, RB + 1):
            a = b + step
            (above if a < 0 else below if a >= EDGE else blur)[a % EDGE, b] += taps[step + RB]
    wide = np.concatenate([interp @ blur] * 2, 0)
    t["across"] = np.concatenate(high_low(wide), 0)
    side = np.concatenate([np.arange(RB), np.arange(EDGE - RB, EDGE)])
    own = np.zeros((128 * USED, 256))
    for g in range(USED):
        own[128 * g : 128 * (g + 1), 16 * g : 16 * (g + 1)] = wide[:, side]
    t["own"] = bf16(own)
    inside = np.zeros((4 * EDGE, 256))
    for i in range(4):
        r, c = slice(EDGE * i, EDGE * (i + 1)), 32 * i
        inside[r, c : c + 32] = cos / 16.0
        inside[r, 128 + c : 128 + c + 32] = -sin / 16.0
        inside[EDGE * i + side] = 0.0
    t["inside"] = bf16(inside)
    rim = np.zeros((256, 768))
    for g in range(USED):
        rim[16 * g : 16 * (g + 1), 32 * g : 32 * g + 32] = cos[side] / 16.0
        rim[16 * g : 16 * (g + 1), 384 + 32 * g : 384 + 32 * g + 32] = -sin[side] / 16.0
    t["rim"] = bf16(rim)
    e_cos, e_sin = waves(side)
    inv_side = np.zeros((256, 128))
    for i in range(4):
        r, c = slice(32 * i, 32 * i + 32), 32 * i
        inv_side[r, c : c + 16] = e_cos.T
        inv_side[r, c + 16 : c + 32] = e_sin.T
        r = slice(128 + 32 * i, 128 + 32 * i + 32)
        inv_side[r, c : c + 16] = -e_sin.T
        inv_side[r, c + 16 : c + 32] = e_cos.T
    t["inv_side"] = bf16(inv_side)
    reach = np.zeros((512, 256))
    for n in range(512):
        q = n % 16
        if n % 256 >= 128 + 128 or (n % 256 >= 128 and (n // 16) % 2):
            continue
        for p in range(16):
            if n < 256 and q >= 8 and p < 8:
                reach[n, p::16] = above[EDGE - RB + q - 8, p]
            if n >= 256 and q < 8 and p >= 8:
                reach[n, p::16] = below[q, EDGE - RB + p - 8]
    t["reach"] = bf16(reach)
    main_high, main_low = high_low((interp @ blur).T)
    t["tall"] = np.concatenate(
        [main_high, bf16((interp @ above).T), bf16((interp @ below).T), main_low], 1
    )
    down = np.zeros((ROWS, EXT))
    for r in range(ROWS):
        down[r, r : r + 2 * RB + 1] = taps
    t["down"] = np.concatenate(high_low(down), 0)
    return t


def dot(a, b):
    return jnp.dot(a, b, preferred_element_type=F32)


def lane_block(width, size):
    return lax.broadcasted_iota(jnp.int32, (1, width), 1) // size


def four_slots(blocks, place):
    total = blocks[0]
    for i in range(1, 4):
        total = jnp.where(place == i, blocks[i], total)
    return total


def start_kernel(mask_hbm, target_hbm, cols_hbm, y_ref, mask_ref, target_ref, cols_ref, sems):
    copies = [
        pltpu.make_async_copy(mask_hbm.at[pl.ds(0, USED)], mask_ref, sems.at[0]),
        pltpu.make_async_copy(cols_hbm, cols_ref, sems.at[1]),
        pltpu.make_async_copy(target_hbm.at[pl.ds(0, USED)], target_ref, sems.at[2]),
    ]
    for copy in copies:
        copy.start()
    copies[0].wait()
    copies[1].wait()
    of_mask = dot(mask_ref[...].reshape(USED * ROWS, EDGE), cols_ref[...])
    copies[2].wait()
    of_target = dot(target_ref[...].reshape(USED * ROWS, EDGE), cols_ref[...])
    place = lane_block(256, 32) % 4
    for n, both in enumerate((of_mask, of_mask + STEP_GAIN * of_target)):
        for j in range(GROUPS):
            firsts = [(4 * j + i) * ROWS for i in range(4)]
            total = four_slots([both[f : f + ROWS] for f in firsts], place).astype(BF)
            lane = 768 * n + 128 * j
            y_ref[:, lane : lane + 128] = total[:, :128]
            y_ref[:, lane + 384 : lane + 512] = total[:, 128:]


def lay_kernels(plane_ref, kernels_ref):
    kernels_ref[...] = jnp.zeros_like(kernels_ref)
    for k in range(NK):
        for part in range(2):
            kernels_ref[k, part, :KF, :KF] = plane_ref[pl.ds(2 * KF * k + part, KF, stride=2), :]
    for k in range(NK):
        for part in range(2):
            one = kernels_ref[k, part]
            one = one + pltpu.roll(one, 32, 1)
            kernels_ref[k, part] = one + pltpu.roll(one, 64, 1)


def slot_lanes(dose_ref, row_ref, joined_block, weight_block):
    up, down, weight = (jnp.zeros(block.shape, F32) for block in (joined_block, joined_block, weight_block))
    rows, doses = row_ref[...], dose_ref[...]
    for g in range(USED):
        row = rows[:, g : g + 1]
        scale = jnp.where(row >= 0, doses[:, g : g + 1], 0.0) * (1.0 / (NK * KF * KF))
        weight = jnp.where(weight_block == g, scale, weight)
        if g > 0:
            before = rows[:, g - 1 : g]
            joined = jnp.where((before >= 0) & (row >= 0) & (before == row - 1), 1.0, 0.0)
            up = jnp.where(joined_block == g, joined, up)
            down = jnp.where(joined_block == g - 1, joined, down)
    return up, down, weight


def lay_narrow(dose_ref, row_ref, narrow_ref):
    up, down, weight = slot_lanes(dose_ref, row_ref, lane_block(256, 2 * RB), lane_block(128 * GROUPS, 32))
    narrow_ref[0:1, :256] = up
    narrow_ref[1:2, :256] = down
    narrow_ref[2:3, :] = weight


def lay_wide(dose_ref, row_ref, slot_ref):
    wide = lane_block(128 * USED, 128)
    up, down, weight = slot_lanes(dose_ref, row_ref, wide, wide)
    slot_ref[0:1, :] = weight
    slot_ref[1:2, :] = up
    slot_ref[2:3, :] = down


def lay_pick(side_ref, reach_ref, pick_ref):
    narrow = lane_block(256, 2 * RB)
    row = lax.broadcasted_iota(jnp.int32, (256, 1), 0)
    source = jnp.where(row < 128, row // 32 + 4 * ((row // 16) % 2), 8 + (row - 128) // 32)
    sources = side_ref[...]
    for n in range(2):
        wanted = jnp.full((1, 256), -1, jnp.int32)
        for g in range(USED):
            wanted = jnp.where(narrow == g, sources[n : n + 1, g : g + 1], wanted)
        rows = slice(256 * n, 256 * (n + 1))
        pick_ref[rows, :] = jnp.where(source == wanted, reach_ref[rows, :].astype(F32), 0.0).astype(BF)


def side_columns(inner, kernels_ref, points, inv_side_ref, narrow_ref, held, bands_ref):
    count = points.shape[0] // 2
    half = 32 * USED
    sides = []
    for j in range(GROUPS):
        lanes, more = slice(128 * j, 128 * (j + 1)), slice(half + 128 * j, half + 128 * (j + 1))
        re = inner[:32, lanes] + inner[32:, more]
        im = inner[:32, more] - inner[32:, lanes]
        for k in range(0, NK, 2):
            pair = []
            for n in (k, k + 1):
                k_re, k_im = kernels_ref[n, 0], kernels_ref[n, 1]
                pair.append(jnp.concatenate([k_re * re - k_im * im, k_re * im + k_im * re], 0).astype(BF))
            both = dot(points, jnp.concatenate(pair, 1)).astype(BF)
            for n in range(2):
                rows, lane = slice((k + n) * count, (k + n + 1) * count), 128 * n
                held[j, rows, :128] = both[:count, lane : lane + 128]
                held[j, rows, 128:] = both[count:, lane : lane + 128]
        field = dot(held[j], inv_side_ref[...])
        squares = jnp.sum((field * field).reshape(NK, count, 128), axis=0)
        sides.append((squares + pltpu.roll(squares, 112, 1)) * narrow_ref[2:3, lanes])
    even = lane_block(128, 16) % 2 == 0
    bands_ref[:, :128] = jnp.where(even, sides[0], pltpu.roll(sides[1], 16, 1)).astype(BF)
    bands_ref[:, 128:] = jnp.where(even, sides[2], 0.0).astype(BF)


def coarse_group(held, j, count, inv_ref, slot_ref):
    field = dot(held[j], inv_ref[...])
    squares = jnp.sum((field * field).reshape(NK, count, 512), axis=0)
    return squares * slot_ref[0:1, 512 * j : 512 * (j + 1)]


def first_kernel(all_ref, rows_ref, plane_ref, grid_ref, inv_side_ref, dose_ref, row_ref,
                 held_ref, bands_ref, kernels_ref, narrow_ref):
    lay_kernels(plane_ref, kernels_ref)
    lay_narrow(dose_ref, row_ref, narrow_ref)
    inner = dot(rows_ref[...], all_ref[:, :768])
    side_columns(inner, kernels_ref, grid_ref[...], inv_side_ref, narrow_ref, held_ref, bands_ref)


def inside_kernel(held_ref, inv_ref, dose_ref, row_ref, tall_ref, across_ref, rows_ref, inside_ref, all_ref, own_ref,
                  reach_ref, side_ref, part_ref, edge_ref, mine_ref, pick_ref, slot_ref, cells_ref, blurred, resist_ref):
    lay_wide(dose_ref, row_ref, slot_ref)
    lay_pick(side_ref, reach_ref, pick_ref)
    for j in range(GROUPS):
        cells_ref[:, 512 * j : 512 * (j + 1)] = coarse_group(held_ref, j, COARSE, inv_ref, slot_ref)
    cells = cells_ref[...]
    lanes = 128 * USED
    above = jnp.concatenate([cells[:, lanes - 128 :], cells[:, : lanes - 128]], 1) * slot_ref[1:2, :]
    below = jnp.concatenate([cells[:, 128:], cells[:, :128]], 1) * slot_ref[2:3, :]
    main = cells.astype(BF)
    edge_ref[...] = dot(main, own_ref[...])
    blurred[...] = dot(tall_ref[...], jnp.concatenate([main, above.astype(BF), below.astype(BF), main], 0)).astype(BF)
    first = pl.multiple_of(lax.axis_index("segment") * ROWS, ROWS)
    mine_ref[...] = blurred[pl.ds(first, ROWS), :]
    for g in range(USED):
        one = blurred[:, 128 * g : 128 * (g + 1)]
        fine = dot(jnp.concatenate([one, one], 1), across_ref[...])
        resist_ref[:, EDGE * g : EDGE * (g + 1)] = resist_of(fine).astype(BF)
    half = 32 * USED
    for j in range(GROUPS):
        change = dot(resist_ref[:, 4 * EDGE * j : 4 * EDGE * (j + 1)], inside_ref[...])
        firsts = (128 * j, half + 128 * j)
        before = jnp.concatenate([all_ref[:, 768 + f : 896 + f] for f in firsts], 1)
        y_part = (before.astype(F32) - STEP_GAIN * change).astype(BF)
        total = dot(rows_ref[...], y_part)
        for n, f in enumerate(firsts):
            part_ref[:, f : f + 128] = total[:, 128 * n : 128 * (n + 1)]


def lent(near_ref, far_ref, pick_ref):
    odd = lax.axis_index("tile") % 2 == 1
    far, near = far_ref[...].astype(F32), near_ref[...].astype(F32)
    left, right = jnp.where(odd, near, far), jnp.where(odd, far, near)
    return dot(jnp.concatenate([left, right], 1).astype(BF), pick_ref[...])


def second_kernel(near_ref, far_ref, pick_ref, edge_ref, narrow_ref, tall_ref, rows_ref, rim_ref, part_ref,
                  kernels_ref, ext_ref, inv_side_ref, held_ref, bands_ref, mine_side_ref, blurred):
    cells = edge_ref[...] + lent(near_ref, far_ref, pick_ref)
    above = pltpu.roll(cells, 2 * RB, 1) * narrow_ref[0:1, :256]
    below = pltpu.roll(cells, 256 - 2 * RB, 1) * narrow_ref[1:2, :256]
    main = cells.astype(BF)
    fine = dot(tall_ref[...], jnp.concatenate([main, above.astype(BF), below.astype(BF), main], 0))
    blurred[...] = fine
    first = pl.multiple_of(lax.axis_index("segment") * ROWS, ROWS)
    mine_side_ref[...] = blurred[pl.ds(first, ROWS), :]
    turned = dot(rows_ref[...], resist_of(fine).astype(BF)).astype(BF)
    inner = part_ref[...] - STEP_GAIN * dot(turned, rim_ref[...])
    ext = ext_ref[pl.ds(first, EXT), :]
    points = jnp.concatenate([ext[:, :64], ext[:, 64:]], 0)
    side_columns(inner, kernels_ref, points, inv_side_ref, narrow_ref, held_ref, bands_ref)


def resist_of(blurred):
    return 0.5 * jnp.tanh((0.5 * STEEPNESS) * (blurred - THRESHOLD)) + 0.5


def stacked(low):
    stack = jnp.concatenate([low[:, 128 * g : 128 * (g + 1)] for g in range(USED)], 0)
    return jnp.concatenate([stack, stack], 1)


def blur_rows(cells, up, down, step, down_ref):
    segment = lax.axis_index("segment")
    width = cells.shape[1]
    top, center, bottom = cells[:RB], cells[RB : RB + ROWS], cells[RB + ROWS :]
    top = jnp.where(segment == 0, pltpu.roll(top, step, 1) * up, top)
    bottom = jnp.where(
        segment == lax.axis_size("segment") - 1, pltpu.roll(bottom, width - step, 1) * down, bottom
    )
    both = dot(down_ref[...], jnp.concatenate([top, center, bottom], 0).astype(BF))
    return both[:ROWS] + both[ROWS:]


def at_sides(narrow, g):
    part = narrow[:, 128 * (g // 8) : 128 * (g // 8) + 128]
    first = 2 * RB * (g % 8)
    return pltpu.roll(part, (128 - first) % 128, 1), pltpu.roll(part, (112 - first) % 128, 1)


def local_kernel(mine_ref, mine_side_ref, held_ref, inv_ref, slot_ref, down_ref, across_ref, mask_ref, target_ref,
                 inner_ref, once_ref, cells_ref):
    fine = dot(stacked(mine_ref[...]), across_ref[...])
    lane = lax.broadcasted_iota(jnp.int32, (1, 128), 1)
    mine_side = mine_side_ref[...]
    for g in range(SLOTS):
        if g < USED:
            left, right = at_sides(mine_side, g)
            part = fine[ROWS * g : ROWS * (g + 1)]
            left = jnp.where(lane < RB, left, part[:, :128])
            right = jnp.where(lane >= 128 - RB, right, part[:, 128:])
            part = jnp.concatenate([left, right], 1)
        else:
            part = jnp.zeros((ROWS, EDGE), F32)
        step = STEP_GAIN * (target_ref[g].astype(F32) - resist_of(part))
        once_ref[g] = (mask_ref[g].astype(F32) + step).astype(BF)
    for j in range(GROUPS):
        cells_ref[:, 512 * j : 512 * (j + 1)] = coarse_group(held_ref, j, EXT, inv_ref, slot_ref)
    low = blur_rows(cells_ref[...], slot_ref[1:2, :], slot_ref[2:3, :], 128, down_ref)
    inner_ref[...] = dot(stacked(low.astype(BF)), across_ref[...])


def final_kernel(inner_ref, near_ref, far_ref, pick_ref, narrow_ref, down_ref, once_ref, target_ref,
                 mask_hbm, resist_hbm, mask_ref, resist_ref, sems):
    def sent(n):
        four = pl.ds(4 * n, 4)
        return [
            pltpu.make_async_copy(resist_ref.at[four], resist_hbm.at[four], sems.at[n]),
            pltpu.make_async_copy(mask_ref.at[four], mask_hbm.at[four], sems.at[4 + n]),
        ]

    lane = lax.broadcasted_iota(jnp.int32, (1, 128), 1)
    for n in (3, 0, 1, 2):
        if n == 0:
            narrow = blur_rows(lent(near_ref, far_ref, pick_ref), narrow_ref[0:1, :256],
                               narrow_ref[1:2, :256], 2 * RB, down_ref)
        for g in range(4 * n, 4 * n + 4):
            if g < USED:
                left, right = at_sides(narrow, g)
                left = jnp.where(lane < RB, left, 0.0)
                right = jnp.where(lane >= 128 - RB, right, 0.0)
                part = inner_ref[ROWS * g : ROWS * (g + 1), :] + jnp.concatenate([left, right], 1)
            else:
                part = jnp.zeros((ROWS, EDGE), F32)
            part = resist_of(part)
            resist_ref[g] = part
            mask_ref[g] = (once_ref[g].astype(F32) + STEP_GAIN * (target_ref[g].astype(F32) - part)).astype(BF)
        for copy in sent(n):
            copy.start()
    for n in range(4):
        for copy in sent(n):
            copy.wait()


VMEM = pl.BlockSpec(memory_space=pltpu.VMEM)
HBM = pl.BlockSpec(memory_space=pltpu.HBM)


def call(kernel, ins, outs, flops, scratch=(), name=None, place=VMEM, grant=32 * 2**20):
    size = sum(math.prod(o.shape) * o.dtype.itemsize for o in outs)
    return pl.pallas_call(
        kernel,
        out_shape=tuple(outs),
        in_specs=list(ins),
        out_specs=tuple(place for _ in outs),
        scratch_shapes=list(scratch),
        compiler_params=pltpu.CompilerParams(vmem_limit_bytes=grant),
        cost_estimate=pl.CostEstimate(flops=flops, bytes_accessed=2 * size, transcendentals=0),
        name=name,
    )


def swapped(block, first):
    pairs = [(i, i + 1) for i in range(first, lax.axis_size("tile") - 1, 2)]
    return lax.ppermute(block, "tile", pairs + [(j, i) for i, j in pairs])


def body(mask, target, spectra, dose, slot_row, side_source):
    t = {name: jnp.asarray(value) for name, value in tables().items()}
    shape = jax.ShapeDtypeStruct
    tile_rows = pltpu.VMEM((USED, ROWS, EDGE), BF)
    plane = spectra.transpose(0, 2, 1, 3).reshape(NK * KF * 2, KF)
    (y,) = call(
        start_kernel,
        [HBM] * 3,
        [shape((ROWS, 128 * USED), BF)],
        10**8,
        [tile_rows, tile_rows, pltpu.VMEM((EDGE, 256), BF), pltpu.SemaphoreType.DMA((3,))],
        name="start",
        grant=62 * 2**20,
    )(mask, target, t["cols"])
    rows_all = lax.all_gather(y, "segment", axis=0, tiled=True)
    doses, rows = dose.reshape(1, SLOTS), slot_row.reshape(1, SLOTS)
    held, bands, kernels, narrow = call(
        first_kernel,
        [VMEM] * 7,
        [
            shape((GROUPS, NK * COARSE, 256), BF),
            shape((COARSE, 256), BF),
            shape((NK, 2, 32, 128), F32),
            shape((8, 128 * GROUPS), F32),
        ],
        10**9,
        name="first",
    )(rows_all, t["rows"], plane, t["grid"], t["inv_side"], doses, rows)
    from_near = swapped(bands, 0)
    from_far = swapped(bands, 1)
    part, edge, mine, pick, slot = call(
        inside_kernel,
        [VMEM] * 12,
        [
            shape((64, 64 * USED), F32),
            shape((COARSE, 256), F32),
            shape((ROWS, 128 * USED), BF),
            shape((512, 256), BF),
            shape((8, 128 * USED), F32),
        ],
        10**9,
        [
            pltpu.VMEM((COARSE, 128 * USED), F32),
            pltpu.VMEM((EDGE, 128 * USED), BF),
            pltpu.VMEM((EDGE, EDGE * USED), BF),
        ],
        name="inside",
    )(held, t["inv"], doses, rows, t["tall"], t["across"], t["rows"], t["inside"], rows_all, t["own"], t["reach"], side_source.T)
    held, bands, mine_side = call(
        second_kernel,
        [VMEM] * 12,
        [shape((GROUPS, NK * EXT, 256), BF), shape((EXT, 256), BF), shape((ROWS, 256), F32)],
        10**9,
        [pltpu.VMEM((EDGE, 256), F32)],
        name="second",
    )(from_near, from_far, pick, edge, narrow, t["tall"], t["rows"], t["rim"], part, kernels, t["ext"], t["inv_side"])
    from_near = swapped(bands, 0)
    from_far = swapped(bands, 1)
    inner, once = call(
        local_kernel,
        [VMEM] * 9,
        [shape((USED * ROWS, EDGE), F32), shape((SLOTS, ROWS, EDGE), BF)],
        10**9,
        [pltpu.VMEM((EXT, 128 * USED), F32)],
        name="local",
    )(mine, mine_side, held, t["inv"], slot, t["down"], t["across"], mask, target)
    return call(
        final_kernel,
        [VMEM] * 8,
        [shape((SLOTS, ROWS, EDGE), BF), shape((SLOTS, ROWS, EDGE), F32)],
        10**8,
        [
            pltpu.VMEM((SLOTS, ROWS, EDGE), BF),
            pltpu.VMEM((SLOTS, ROWS, EDGE), F32),
            pltpu.SemaphoreType.DMA((8,)),
        ],
        name="final",
        place=HBM,
    )(inner, from_near, from_far, pick, narrow, t["down"], once, target)


def solution(mesh):
    in_specs = (
        P("tile", "segment", None),
        P("tile", "segment", None),
        P(),
        P("tile"),
        P("tile"),
        P("tile", None),
    )
    out_specs = (P("tile", "segment", None), P("tile", "segment", None))
    return jax.shard_map(body, mesh=mesh, in_specs=in_specs, out_specs=out_specs, check_vma=False)
```
